256 devices in a mesh: ka: 64 (over x, y, z_hi, core), ot: 4 (over z_lo).
Axes of the slice: x: 4, y: 4, z: 8 (z_hi: 2, z_lo: 4; z = z_hi * 4 + z_lo), core: 2. Of those that a mesh axis runs over, the one named last changes fastest.
Arguments:
- green_coeff: bfloat16 [2304, 128, 128], P('ka', 'ot'), may hold values from -6 to 6
- screened: bfloat16 [2304, 256, 256], P(None, ('ot', 'ka')), may hold values from -6 to 6
- band_energy: float32 [2304, 2], P('ka'), may hold values from -4 to 4
- time_basis: float32 [64, 128], replicated, may hold values from -0.75 to 0.75
- projector: float32 [128, 64], replicated, may hold values from -0.5 to 0.5
- memory_kernel: float32 [64, 64], replicated, may hold values from -0.09375 to 0.09375
Outputs:
- sigma_coeff: bfloat16 [2304, 128, 128], P('ka', 'ot')
- green_next: bfloat16 [2304, 128, 128], P('ka', 'ot')
The draws below stay inside these ranges and needn't reach their ends.
All inputs are finite; a program needn't handle non-finite values.
Results may differ from the reference program's by a relative error of at most 0.013.
Values may be sent and summed in bfloat16 or wider, within the bound.
A program may use at most 64 MiB of HBM per device.

```python
import math
import jax
import jax.numpy as jnp
from jax import lax

LAT = 48
NK = 2304
ORB = 2
NB = 64
NQ = 128
STEPS = 1


def block_levels(key, extent, pieces, low, largest):
    gain, own = 1.0, jax.random.fold_in(key, 6)
    for dim, parts in pieces:
        draws = jnp.exp(jax.random.uniform(jax.random.fold_in(own, dim), (parts,), jnp.float32, low / len(pieces), largest / len(pieces)))
        gain = gain * jnp.repeat(draws, extent[dim] // parts).reshape([-1 if axis == dim else 1 for axis in range(len(extent))])
    return gain


def bell_draw(rng, extent, spread, limit, pieces=(), kind=jnp.bfloat16):
    array = jax.random.normal(rng, extent, jnp.float32) * spread
    if len(pieces) > 0:
        array = block_levels(rng, extent, pieces, -0.22, 0.18) * array
    return jnp.clip(array, min=-limit, max=limit).astype(kind)


def setup_inputs(seed: int = 0) -> dict:
    keys = jax.random.split(jax.random.key(seed), 7)
    green_coeff = bell_draw(keys[0], (NK, ORB * NB, 2 * NB), 1.0, 6.0, ((0, 64), (1, 4)))
    screened = bell_draw(keys[1], (NK, ORB * NQ, 2 * NQ), 1.0, 6.0, ((1, 256),))
    band_energy = jnp.clip(jax.random.uniform(keys[2], (NK, ORB), jnp.float32, -4.0, 4.0) * block_levels(keys[2], (NK, ORB), ((0, 64),), -0.4, 0.0), -4.0, 4.0)
    time_basis = bell_draw(keys[3], (NB, NQ), NB ** -0.5, 0.75, (), jnp.float32)
    projector = bell_draw(keys[4], (NQ, NB), NQ ** -0.5, 0.5, (), jnp.float32)
    memory_kernel = bell_draw(keys[5], (NB, NB), (NB * NB) ** -0.5, 0.09375, (), jnp.float32)
    return {"green_coeff": green_coeff, "screened": screened, "band_energy": band_energy, "time_basis": time_basis, "projector": projector, "memory_kernel": memory_kernel}


STEP_SIZE = 0.25
PRECISE = lax.Precision.HIGHEST


def sigma_of(coeff_re, coeff_im, screen_part, time_basis, projector):
    qblock = math.gcd(NQ, 16)
    blocks = NQ // qblock

    def one_block(totals, block_index):
        offset = (block_index * qblock).astype(jnp.int32)
        basis_part = lax.dynamic_slice_in_dim(time_basis, offset, qblock, 1)
        rows_re = jnp.einsum('kml,lq->kmq', coeff_re, basis_part, precision=PRECISE)
        rows_im = jnp.einsum('kml,lq->kmq', coeff_im, basis_part, precision=PRECISE)
        val_re = jnp.einsum('kmq,mj->kqj', rows_re, time_basis, precision=PRECISE)
        val_im = jnp.einsum('kmq,mj->kqj', rows_im, time_basis, precision=PRECISE)
        val_re = lax.optimization_barrier(val_re.astype(jnp.bfloat16)).astype(jnp.float32)
        val_im = lax.optimization_barrier(val_im.astype(jnp.bfloat16)).astype(jnp.float32)
        grid_vals = lax.complex(val_re, val_im).reshape(LAT, LAT, qblock, NQ)
        near_field = jnp.fft.ifft2(grid_vals, axes=(0, 1))
        wave_part = lax.dynamic_slice_in_dim(screen_part, offset, qblock, 1).astype(jnp.float32)
        wave_cplx = lax.complex(wave_part[..., :NQ], wave_part[..., NQ:]).reshape(LAT, LAT, qblock, NQ)
        far_field = 1j * near_field * wave_cplx
        back_field = jnp.fft.fft2(far_field, axes=(0, 1)).reshape(NK, qblock, NQ)
        proj_part = lax.dynamic_slice_in_dim(projector, offset, qblock, 0)
        home_re = jnp.einsum('kqj,jm->kqm', jnp.real(back_field), projector, precision=PRECISE)
        home_im = jnp.einsum('kqj,jm->kqm', jnp.imag(back_field), projector, precision=PRECISE)
        add_re = jnp.einsum('kqm,qn->kmn', home_re, proj_part, precision=PRECISE)
        add_im = jnp.einsum('kqm,qn->kmn', home_im, proj_part, precision=PRECISE)
        return (totals[0] + add_re, totals[1] + add_im), None

    start_sums = (jnp.zeros((NK, NB, NB), jnp.float32), jnp.zeros((NK, NB, NB), jnp.float32))
    totals, unused = lax.scan(one_block, start_sums, jnp.arange(blocks, dtype=jnp.int32))
    return totals


def reference(green_coeff, screened, band_energy, time_basis, projector, memory_kernel):
    current = green_coeff
    sigma_all = green_coeff
    for step_index in range(STEPS):
        sigma_rows = []
        next_rows = []
        for orbital in range(ORB):
            coeffs = current[:, orbital * NB:(orbital + 1) * NB, :].astype(jnp.float32)
            coeff_re = coeffs[:, :, :NB]
            coeff_im = coeffs[:, :, NB:]
            screen_part = screened[:, orbital * NQ:(orbital + 1) * NQ, :]
            sum_re, sum_im = sigma_of(coeff_re, coeff_im, screen_part, time_basis, projector)
            sigma_bf = jnp.concatenate([sum_re, sum_im], axis=2).astype(jnp.bfloat16)
            sigma_f32 = lax.optimization_barrier(sigma_bf).astype(jnp.float32)
            kern_re = jnp.einsum('kmn,np->kmp', sigma_f32[:, :, :NB], memory_kernel, precision=PRECISE)
            kern_im = jnp.einsum('kmn,np->kmp', sigma_f32[:, :, NB:], memory_kernel, precision=PRECISE)
            mem_re = jnp.einsum('kmp,kpl->kml', kern_re, coeff_re, precision=PRECISE) - jnp.einsum('kmp,kpl->kml', kern_im, coeff_im, precision=PRECISE)
            mem_im = jnp.einsum('kmp,kpl->kml', kern_re, coeff_im, precision=PRECISE) + jnp.einsum('kmp,kpl->kml', kern_im, coeff_re, precision=PRECISE)
            energy = band_energy[:, orbital][:, None, None]
            next_re = coeff_re + STEP_SIZE * (energy * coeff_im + mem_im)
            next_im = coeff_im - STEP_SIZE * (energy * coeff_re + mem_re)
            next_rows.append(jnp.concatenate([next_re, next_im], axis=2).astype(jnp.bfloat16))
            sigma_rows.append(sigma_bf)
        current = jnp.concatenate(next_rows, axis=1)
        sigma_all = jnp.concatenate(sigma_rows, axis=1)
    return sigma_all, current
```

```python
import functools
import math

import jax
import jax.numpy as jnp
import numpy as np
from jax import lax
from jax.experimental import pallas as pl
from jax.experimental.pallas import tpu as pltpu
from jax.sharding import PartitionSpec as P

STEP_SIZE = 0.25
MESH = pl.DeviceIdType.MESH
BF = jnp.bfloat16
F32 = jnp.float32
PAD = 24


def phase_tables(lattice, block, group):
    kx_rows = group * block // lattice
    half = block // 2
    cosine = lambda a, b: np.cos(2.0 * math.pi * (a * b % lattice) / lattice)
    sine = lambda a, b: np.sin(2.0 * math.pi * (a * b % lattice) / lattice)
    idx = np.arange(lattice)
    cx, sx = cosine(idx[:, None], idx[None, :]), sine(idx[:, None], idx[None, :])
    x_fwd = np.concatenate([cx, sx], axis=1)
    x_inv = np.concatenate([cx, -sx], axis=1)
    row = np.arange(group * 2 * PAD)
    place, inner = row // PAD, row % PAD
    kk = (place // 2) * block + (place % 2) * half + inner
    valid = inner < half
    kx_of, ky_of = kk // lattice, kk % lattice
    lat_row = np.arange(kx_rows * lattice)
    rx_of, ry_of = lat_row // lattice, lat_row % lattice
    same = (rx_of[:, None] == kx_of[None, :]) & valid[None, :]
    cy = np.where(same, cosine(ry_of[:, None], ky_of[None, :]), 0.0)
    sy = np.where(same, sine(ry_of[:, None], ky_of[None, :]), 0.0)
    y_fwd = np.concatenate([cy, sy], axis=1)
    y_inv = np.concatenate([cy.T, -sy.T], axis=1)
    return [t.astype(np.float32) for t in (x_fwd, x_inv, y_fwd, y_inv)]


def split(value):
    high = value.astype(BF)
    return high, (value - high.astype(F32)).astype(BF)


def dot(left, right):
    return jnp.dot(left, right, preferred_element_type=F32)


def kernel(
    green_ref, screen_ref, energy_ref, basis_ref, proj_ref, memk_ref,
    xf_ref, xi_ref, yf_ref, yi_ref,
    sigma_ref, next_ref,
    w_raw, wre_full, wim_full, pages, packed1, landed1, packed2, landed2, ytab, utab, xbuf,
    tb, pb, pq, kb, pt, partner, gmat, amat, skm,
    wsem, lsem, ssem1, rsem1, ssem2, rsem2, psem, qsem,
):
    ka, ot = lax.axis_index("ka"), lax.axis_index("ot")
    half, orbital = ot % 2, ot // 2
    mine, place = ka // 4, half * 4 + ka % 4
    count_k, rows_m, width = green_ref.shape
    hk = count_k // 2

    def device_of(grp, slot):
        return (grp * 4 + slot % 4, orbital * 2 + slot // 4)

    barrier = pltpu.get_barrier_semaphore()

    def greet(step, carry):
        slot = (place + step) % 8
        grp = (mine + step // 8) % 16
        pl.semaphore_signal(barrier, inc=1, device_id=device_of(grp, slot), device_id_type=MESH)
        return carry

    lax.fori_loop(1, 128, greet, 0)
    w_copy = pltpu.make_async_copy(screen_ref, w_raw, wsem)
    w_copy.start()

    lane64 = lax.broadcasted_iota(jnp.int32, (1, width), 1)
    low64 = lane64 < 64
    low32 = lane64 % 64 < 32
    minus_low = jnp.where(low64, -1.0, 1.0).astype(F32)

    def times_i(value):
        return pltpu.roll(value, 64, 1) * minus_low

    basis_t = basis_ref[...].T
    t_high, t_low = split(basis_t)
    t_cat = jnp.concatenate([t_high, t_low], axis=1)

    def rows_step(r, carry):
        parts = []
        both = [green_ref[r].astype(F32), green_ref[hk + r].astype(F32)]
        turned = [pltpu.roll(v, 64, 1) for v in both]
        for v, u in zip(both, turned):
            parts.append(jnp.where(low64, v, u))
        for v, u in zip(both, turned):
            parts.append(jnp.where(low64, u, v))
        right = jnp.concatenate(parts, axis=0).astype(BF)
        out = lax.dot_general(
            t_cat, right, (((1,), (1,)), ((), ())), preferred_element_type=F32
        )
        pages[pl.ds(r, 128, stride=PAD), :] = out
        return carry

    for r in range(hk):
        rows_step(r, 0)

    pl.semaphore_wait(barrier, 127)

    def send1(t, carry):
        grp = (mine + t) % 16
        for slot in range(8):
            q = (slot // 4) * 64 + grp * 4 + slot % 4
            start = pl.multiple_of(q * PAD, 8)
            value = pages[pl.ds(start, hk), :].astype(BF)
            packed1[grp, slot] = value.reshape(hk // 2, 2, width)
        for slot in range(8):
            @pl.when((t != 0) | (slot != place))
            def _():
                pltpu.make_async_remote_copy(
                    src_ref=packed1.at[grp, slot], dst_ref=landed1.at[mine, place],
                    send_sem=ssem1, recv_sem=rsem1.at[t],
                    device_id=device_of(grp, slot), device_id_type=MESH,
                ).start()
        return carry

    lax.fori_loop(0, 16, send1, 0)
    own1 = pltpu.make_async_copy(packed1.at[mine, place], landed1.at[mine, place], lsem)
    own1.start()

    zeros = jnp.zeros((64, 128), F32)
    basis = basis_ref[...]
    wide = jnp.concatenate(
        [jnp.concatenate([basis, zeros], axis=1), jnp.concatenate([zeros, basis], axis=1)], axis=0
    )
    high, low = split(wide)
    tb[0:128, :] = high
    tb[128:256, :] = low
    proj = proj_ref[...].T
    blank = jnp.zeros((128, 64), F32)
    left, right = jnp.concatenate([proj, blank], axis=1), jnp.concatenate([blank, proj], axis=1)
    for offset, piece in ((0, left), (128, right)):
        high, low = split(piece)
        pb[offset:offset + 128, :] = high
        pb[256 + offset:256 + offset + 128, :] = low
    pt[0:128, :] = left
    for grp in range(16):
        for h in range(2):
            pt[pl.ds(128 + grp * 8 + h * 4, 4), :] = pt[pl.ds(h * 64 + grp * 4, 4), :]
    left = pt[128:256, :]
    right = pltpu.roll(left, 64, 1)
    for offset, piece in ((0, left), (128, right)):
        high, low = split(piece)
        pq[offset:offset + 128, :] = high
        pq[256 + offset:256 + offset + 128, :] = low
    memk = memk_ref[...]
    blank = jnp.zeros((64, 64), F32)
    wide = jnp.concatenate(
        [jnp.concatenate([memk, blank], axis=1), jnp.concatenate([blank, memk], axis=1)], axis=0
    )
    high, low = split(wide)
    kb[0:128, :] = high
    kb[128:256, :] = low
    w_copy.wait()
    scale = 1.0 / w_raw.shape[0]

    def widen(i, carry):
        at = pl.ds(pl.multiple_of(i * 96, 32), 96)
        value = w_raw[at, :].astype(F32) * scale
        wre_full[at, :] = value[:, :128]
        wim_full[at, :] = value[:, 128:]
        return carry

    lax.fori_loop(0, 24, widen, 0)
    xbuf[...] = jnp.zeros_like(xbuf)
    own1.wait()

    def arrive1(t, carry):
        grp = (mine + 16 - t) % 16

        @pl.when(t == 0)
        def _():
            ref = landed1.at[grp, pl.ds(0, 7)]
            pltpu.make_async_copy(ref, ref, rsem1.at[t]).wait()

        @pl.when(t != 0)
        def _():
            ref = landed1.at[grp]
            pltpu.make_async_copy(ref, ref, rsem1.at[t]).wait()

        for i in range(4):
            v0 = landed1[grp, i].reshape(hk, width).astype(F32)
            v1 = landed1[grp, 4 + i].reshape(hk, width).astype(F32)
            xbuf[i * 2 * PAD:i * 2 * PAD + hk, :] = jnp.where(low32, v0, pltpu.roll(v1, 32, 1))
            xbuf[i * 2 * PAD + PAD:i * 2 * PAD + PAD + hk, :] = jnp.where(
                low32, pltpu.roll(v0, 96, 1), v1
            )
        value = xbuf[...]
        stacked = jnp.concatenate([value.astype(BF), times_i(value).astype(BF)], axis=0)
        ytab[pl.ds(pl.multiple_of(grp * 144, 8), 144), :] = dot(yf_ref[...], stacked)
        return carry

    lax.fori_loop(0, 16, arrive1, 0)

    swap = pltpu.make_async_remote_copy(
        src_ref=green_ref, dst_ref=partner, send_sem=psem, recv_sem=qsem,
        device_id=(ka, orbital * 2 + 1 - half), device_id_type=MESH,
    )
    swap.start()

    together = 6

    def distances(step, carry):
        near_in = []
        for u in range(0, together, 2):
            sides = []
            for v in range(2):
                ry = step * together + u + v
                value = ytab[pl.ds(ry, 48, stride=48), :]
                sides.append(
                    jnp.concatenate([value.astype(BF), times_i(value).astype(BF)], axis=0)
                )
            out = dot(xf_ref[...], jnp.concatenate(sides, axis=1)).astype(BF)
            near_in += [out[:, :128], out[:, 128:]]
        near_in = jnp.concatenate(near_in, axis=0)
        near = dot(jnp.concatenate([near_in, near_in], axis=1), tb[...])
        far_parts = []
        for u in range(together):
            ry = step * together + u
            w_re = wre_full[pl.ds(ry, 48, stride=48), :]
            w_im = wim_full[pl.ds(ry, 48, stride=48), :]
            n_re, n_im = near[u * 48:u * 48 + 48, :128], near[u * 48:u * 48 + 48, 128:]
            far_re = -(n_re * w_im + n_im * w_re)
            far_im = n_re * w_re - n_im * w_im
            far_parts.append(jnp.concatenate([far_re.astype(BF), far_im.astype(BF)], axis=1))
        far = jnp.concatenate(far_parts, axis=0)
        home = dot(far, pb[0:256, :]) + dot(far, pb[256:512, :])
        for u in range(0, together, 2):
            sides = []
            for v in range(2):
                value = home[(u + v) * 48:(u + v) * 48 + 48, :]
                sides.append(
                    jnp.concatenate([value.astype(BF), times_i(value).astype(BF)], axis=0)
                )
            out = dot(xi_ref[...], jnp.concatenate(sides, axis=1))
            for v in range(2):
                at = pl.multiple_of((step * together + u + v) * 48, 8)
                utab[pl.ds(at, 48), :] = out[:, v * 128:v * 128 + 128]
        return carry

    lax.fori_loop(0, 48 // together, distances, 0)

    def send2(t, carry):
        grp = (mine + t) % 16
        value = jnp.concatenate(
            [utab[pl.ds(grp * 3 + u, 48, stride=48), :] for u in range(3)], axis=0
        )
        stacked = jnp.concatenate([value.astype(BF), times_i(value).astype(BF)], axis=0)
        out = dot(yi_ref[...], stacked)
        for i in range(4):
            v0 = out[i * 2 * PAD:i * 2 * PAD + PAD]
            v1 = out[i * 2 * PAD + PAD:i * 2 * PAD + 2 * PAD]
            first = jnp.where(low32, v0, pltpu.roll(v1, 32, 1))
            second = jnp.where(low32, pltpu.roll(v0, 96, 1), v1)
            packed2[grp, i] = first[:hk].astype(BF).reshape(hk // 2, 2, width)
            packed2[grp, 4 + i] = second[:hk].astype(BF).reshape(hk // 2, 2, width)
        for slot in range(8):
            @pl.when((t != 0) | (slot != place))
            def _():
                pltpu.make_async_remote_copy(
                    src_ref=packed2.at[grp, slot], dst_ref=landed2.at[mine, place],
                    send_sem=ssem2, recv_sem=rsem2.at[t],
                    device_id=device_of(grp, slot), device_id_type=MESH,
                ).start()
        return carry

    lax.fori_loop(0, 16, send2, 0)
    own2 = pltpu.make_async_copy(packed2.at[mine, place], landed2.at[mine, place], lsem)
    own2.start()

    swap.wait()
    mine_at = pl.multiple_of(half * rows_m, 32)
    other_at = pl.multiple_of((1 - half) * rows_m, 32)

    def build(k, carry):
        for ref, at in ((green_ref, mine_at), (partner, other_at)):
            value = ref[k]
            turned = (pltpu.roll(value.astype(F32), 64, 1) * -minus_low).astype(BF)
            gmat[k, pl.ds(at, rows_m), :] = turned
            gmat[k, pl.ds(64 + at, rows_m), :] = value
        return carry

    lax.fori_loop(0, count_k, build, 0)
    own2.wait()

    def arrive2(t, carry):
        grp = (mine + 16 - t) % 16

        @pl.when(t == 0)
        def _():
            ref = landed2.at[grp, pl.ds(0, 7)]
            pltpu.make_async_copy(ref, ref, rsem2.at[t]).wait()

        @pl.when(t != 0)
        def _():
            ref = landed2.at[grp]
            pltpu.make_async_copy(ref, ref, rsem2.at[t]).wait()

        for slot in range(8):
            value = landed2[grp, slot].reshape(hk, width).astype(F32)
            start = pl.multiple_of((grp * 8 + slot) * PAD, 8)
            pages[pl.ds(start, hk), :] = value
        return carry

    lax.fori_loop(0, 16, arrive2, 0)

    for r in range(hk):
        value = pages[pl.ds(r, 128, stride=PAD), :].T.astype(BF)
        for k2 in range(2):
            amat[(k2 * hk + r) * rows_m:(k2 * hk + r + 1) * rows_m, 0:128] = value[
                k2 * 32:k2 * 32 + 32
            ]
            amat[(k2 * hk + r) * rows_m:(k2 * hk + r + 1) * rows_m, 128:256] = value[
                64 + k2 * 32:64 + k2 * 32 + 32
            ]

    def coeffs(i, carry):
        at = pl.multiple_of(i * 192, 32)
        value = amat[pl.ds(at, 192), :]
        sigma = (dot(value, pq[0:256, :]) + dot(value, pq[256:512, :])).astype(BF)
        sigma_ref[pl.ds(i * 6, 6)] = sigma.reshape(6, rows_m, width)
        skm[pl.ds(at, 192), :] = dot(jnp.concatenate([sigma, sigma], axis=1), kb[...]).astype(BF)
        for u in range(6):
            k = i * 6 + u
            row = pl.multiple_of(i * 192 + u * 32, 32)
            memory = dot(skm[pl.ds(row, rows_m), :], gmat[k])
            turned = gmat[k, pl.ds(mine_at, rows_m), :].astype(F32)
            own = green_ref[k].astype(F32)
            energy = energy_ref[orbital, k]
            next_ref[k] = (own + STEP_SIZE * (energy * turned + memory)).astype(BF)
        return carry

    lax.fori_loop(0, count_k // 6, coeffs, 0)

    ref = landed1.at[pl.ds(0, 15)]
    pltpu.make_async_copy(ref, ref, ssem1).wait()
    ref = landed1.at[0, pl.ds(0, 7)]
    pltpu.make_async_copy(ref, ref, ssem1).wait()
    ref = landed2.at[pl.ds(0, 15)]
    pltpu.make_async_copy(ref, ref, ssem2).wait()
    ref = landed2.at[0, pl.ds(0, 7)]
    pltpu.make_async_copy(ref, ref, ssem2).wait()


def on_device(green_coeff, screened, band_energy, time_basis, projector, memory_kernel):
    total_k = screened.shape[0]
    tables = [jnp.asarray(t, BF) for t in phase_tables(48, green_coeff.shape[0], 4)]
    vmem = pl.BlockSpec(memory_space=pltpu.VMEM)
    dma = pltpu.SemaphoreType.DMA
    message = (16, 8, 9, 2, 128)
    out = jax.ShapeDtypeStruct(green_coeff.shape, BF)
    return pl.pallas_call(
        kernel,
        out_shape=(out, out),
        in_specs=[
            vmem,
            pl.BlockSpec(memory_space=pl.ANY),
            pl.BlockSpec(memory_space=pltpu.SMEM),
            vmem, vmem, vmem, vmem, vmem, vmem, vmem,
        ],
        out_specs=(vmem, vmem),
        scratch_shapes=[
            pltpu.VMEM((total_k, 256), BF),
            pltpu.VMEM((total_k, 128), F32),
            pltpu.VMEM((total_k, 128), F32),
            pltpu.VMEM((128 * PAD, 128), F32),
            pltpu.VMEM(message, BF),
            pltpu.VMEM(message, BF),
            pltpu.VMEM(message, BF),
            pltpu.VMEM(message, BF),
            pltpu.VMEM((total_k, 128), F32),
            pltpu.VMEM((total_k, 128), F32),
            pltpu.VMEM((8 * PAD, 128), F32),
            pltpu.VMEM((256, 256), BF),
            pltpu.VMEM((512, 128), BF),
            pltpu.VMEM((512, 128), BF),
            pltpu.VMEM((256, 128), BF),
            pltpu.VMEM((256, 128), F32),
            pltpu.VMEM(green_coeff.shape, BF),
            pltpu.VMEM((36, 128, 128), BF),
            pltpu.VMEM((1152, 256), BF),
            pltpu.VMEM((1152, 128), BF),
            dma, dma, dma, dma((16,)), dma, dma((16,)), dma, dma,
        ],
        compiler_params=pltpu.CompilerParams(
            collective_id=0, has_side_effects=True, vmem_limit_bytes=48 * 2**20
        ),
    )(
        green_coeff,
        screened.reshape(total_k, 256),
        band_energy.T,
        time_basis,
        projector.T,
        memory_kernel,
        *tables,
    )


def solution(mesh):
    return jax.shard_map(
        on_device,
        mesh=mesh,
        in_specs=(P("ka", "ot", None), P(None, ("ot", "ka"), None), P("ka", None), P(), P(), P()),
        out_specs=(P("ka", "ot", None), P("ka", "ot", None)),
        check_vma=False,
    )
```

```python
import functools
import math

import jax
import jax.numpy as jnp
import numpy as np
from jax import lax
from jax.experimental import pallas as pl
from jax.experimental.pallas import tpu as pltpu
from jax.sharding import PartitionSpec as P

STEP_SIZE = 0.25
MESH = pl.DeviceIdType.MESH
BF = jnp.bfloat16
F32 = jnp.float32
PAD = 24


def phase_tables(lattice, block, group):
    kx_rows = group * block // lattice
    half = block // 2
    cosine = lambda a, b: np.cos(2.0 * math.pi * (a * b % lattice) / lattice)
    sine = lambda a, b: np.sin(2.0 * math.pi * (a * b % lattice) / lattice)
    idx = np.arange(lattice)
    cx, sx = cosine(idx[:, None], idx[None, :]), sine(idx[:, None], idx[None, :])
    x_fwd = np.concatenate([cx, sx], axis=1)
    x_inv = np.concatenate([cx, -sx], axis=1)
    row = np.arange(group * 2 * PAD)
    place, inner = row // PAD, row % PAD
    kk = (place // 2) * block + (place % 2) * half + inner
    valid = inner < half
    kx_of, ky_of = kk // lattice, kk % lattice
    lat_row = np.arange(kx_rows * lattice)
    rx_of, ry_of = lat_row // lattice, lat_row % lattice
    same = (rx_of[:, None] == kx_of[None, :]) & valid[None, :]
    cy = np.where(same, cosine(ry_of[:, None], ky_of[None, :]), 0.0)
    sy = np.where(same, sine(ry_of[:, None], ky_of[None, :]), 0.0)
    y_fwd = np.concatenate([cy, sy], axis=1)
    y_inv = np.concatenate([cy.T, -sy.T], axis=1)
    return [t.astype(np.float32) for t in (x_fwd, x_inv, y_fwd, y_inv)]


def split(value):
    high = value.astype(BF)
    return high, (value - high.astype(F32)).astype(BF)


def dot(left, right):
    return jnp.dot(left, right, preferred_element_type=F32)


def kernel(
    green_in, screen_in, energy_in, basis_in, proj_in, memk_in, xf_in, xi_in, yf_in, yi_in,
    sigma_ref, next_ref,
    green_ref, w_raw, energy_ref, basis_ref, proj_ref, memk_ref, xf_ref, xi_ref, yf_ref, yi_ref,
    fsem, wre_full, wim_full, pages, packed1, landed1, packed2, landed2, ytab, utab, xbuf,
    tb, pb, pq, kb, pt, partner, gmat, amat, skm,
    lsem, ssem1, rsem1, ssem2, rsem2, psem, qsem,
):
    ka, ot = lax.axis_index("ka"), lax.axis_index("ot")
    half, orbital = ot % 2, ot // 2
    mine, place = ka // 4, half * 4 + ka % 4
    count_k, rows_m, width = green_ref.shape
    hk = count_k // 2

    def device_of(grp, slot):
        return (grp * 4 + slot % 4, orbital * 2 + slot // 4)

    barrier = pltpu.get_barrier_semaphore()

    def greet(step, carry):
        slot = (place + step) % 8
        grp = (mine + step // 8) % 16
        pl.semaphore_signal(barrier, inc=1, device_id=device_of(grp, slot), device_id_type=MESH)
        return carry

    fetches = [
        pltpu.make_async_copy(source, target, fsem.at[i])
        for i, (source, target) in enumerate([
            (green_in, green_ref), (basis_in, basis_ref), (screen_in, w_raw),
            (energy_in, energy_ref), (proj_in, proj_ref), (memk_in, memk_ref),
            (xf_in, xf_ref), (xi_in, xi_ref), (yf_in, yf_ref), (yi_in, yi_ref),
        ])
    ]
    for fetch in fetches:
        fetch.start()
    lax.fori_loop(1, 128, greet, 0)
    for fetch in fetches[:2]:
        fetch.wait()

    lane64 = lax.broadcasted_iota(jnp.int32, (1, width), 1)
    low64 = lane64 < 64
    low32 = lane64 % 64 < 32
    minus_low = jnp.where(low64, -1.0, 1.0).astype(F32)

    def times_i(value):
        return pltpu.roll(value, 64, 1) * minus_low

    basis_t = basis_ref[...].T
    t_high, t_low = split(basis_t)
    t_cat = jnp.concatenate([t_high, t_low], axis=1)

    def rows_step(r, carry):
        parts = []
        both = [green_ref[r].astype(F32), green_ref[hk + r].astype(F32)]
        turned = [pltpu.roll(v, 64, 1) for v in both]
        for v, u in zip(both, turned):
            parts.append(jnp.where(low64, v, u))
        for v, u in zip(both, turned):
            parts.append(jnp.where(low64, u, v))
        right = jnp.concatenate(parts, axis=0).astype(BF)
        out = lax.dot_general(
            t_cat, right, (((1,), (1,)), ((), ())), preferred_element_type=F32
        )
        pages[pl.ds(r, 128, stride=PAD), :] = out
        return carry

    for r in range(hk):
        rows_step(r, 0)

    pl.semaphore_wait(barrier, 127)

    def send1(t, carry):
        grp = (mine + t) % 16
        for slot in range(8):
            q = (slot // 4) * 64 + grp * 4 + slot % 4
            start = pl.multiple_of(q * PAD, 8)
            value = pages[pl.ds(start, hk), :].astype(BF)
            packed1[grp, slot] = value.reshape(hk // 2, 2, width)
        for slot in range(8):
            @pl.when((t != 0) | (slot != place))
            def _():
                pltpu.make_async_remote_copy(
                    src_ref=packed1.at[grp, slot], dst_ref=landed1.at[mine, place],
                    send_sem=ssem1, recv_sem=rsem1.at[t],
                    device_id=device_of(grp, slot), device_id_type=MESH,
                ).start()
        return carry

    lax.fori_loop(0, 16, send1, 0)
    own1 = pltpu.make_async_copy(packed1.at[mine, place], landed1.at[mine, place], lsem)
    own1.start()

    for fetch in fetches[2:]:
        fetch.wait()
    zeros = jnp.zeros((64, 128), F32)
    basis = basis_ref[...]
    wide = jnp.concatenate(
        [jnp.concatenate([basis, zeros], axis=1), jnp.concatenate([zeros, basis], axis=1)], axis=0
    )
    high, low = split(wide)
    tb[0:128, :] = high
    tb[128:256, :] = low
    proj = proj_ref[...].T
    blank = jnp.zeros((128, 64), F32)
    left, right = jnp.concatenate([proj, blank], axis=1), jnp.concatenate([blank, proj], axis=1)
    for offset, piece in ((0, left), (128, right)):
        high, low = split(piece)
        pb[offset:offset + 128, :] = high
        pb[256 + offset:256 + offset + 128, :] = low
    pt[0:128, :] = left
    for grp in range(16):
        for h in range(2):
            pt[pl.ds(128 + grp * 8 + h * 4, 4), :] = pt[pl.ds(h * 64 + grp * 4, 4), :]
    left = pt[128:256, :]
    right = pltpu.roll(left, 64, 1)
    for offset, piece in ((0, left), (128, right)):
        high, low = split(piece)
        pq[offset:offset + 128, :] = high
        pq[256 + offset:256 + offset + 128, :] = low
    memk = memk_ref[...]
    blank = jnp.zeros((64, 64), F32)
    wide = jnp.concatenate(
        [jnp.concatenate([memk, blank], axis=1), jnp.concatenate([blank, memk], axis=1)], axis=0
    )
    high, low = split(wide)
    kb[0:128, :] = high
    kb[128:256, :] = low
    scale = 1.0 / w_raw.shape[0]

    def widen(i, carry):
        at = pl.ds(pl.multiple_of(i * 96, 32), 96)
        value = w_raw[at, :].astype(F32) * scale
        wre_full[at, :] = value[:, :128]
        wim_full[at, :] = value[:, 128:]
        return carry

    lax.fori_loop(0, 24, widen, 0)
    xbuf[...] = jnp.zeros_like(xbuf)
    own1.wait()

    def arrive1(t, carry):
        grp = (mine + 16 - t) % 16

        @pl.when(t == 0)
        def _():
            ref = landed1.at[grp, pl.ds(0, 7)]
            pltpu.make_async_copy(ref, ref, rsem1.at[t]).wait()

        @pl.when(t != 0)
        def _():
            ref = landed1.at[grp]
            pltpu.make_async_copy(ref, ref, rsem1.at[t]).wait()

        for i in range(4):
            v0 = landed1[grp, i].reshape(hk, width).astype(F32)
            v1 = landed1[grp, 4 + i].reshape(hk, width).astype(F32)
            xbuf[i * 2 * PAD:i * 2 * PAD + hk, :] = jnp.where(low32, v0, pltpu.roll(v1, 32, 1))
            xbuf[i * 2 * PAD + PAD:i * 2 * PAD + PAD + hk, :] = jnp.where(
                low32, pltpu.roll(v0, 96, 1), v1
            )
        value = xbuf[...]
        stacked = jnp.concatenate([value.astype(BF), times_i(value).astype(BF)], axis=0)
        ytab[pl.ds(pl.multiple_of(grp * 144, 8), 144), :] = dot(yf_ref[...], stacked)
        return carry

    lax.fori_loop(0, 16, arrive1, 0)

    swap = pltpu.make_async_remote_copy(
        src_ref=green_ref, dst_ref=partner, send_sem=psem, recv_sem=qsem,
        device_id=(ka, orbital * 2 + 1 - half), device_id_type=MESH,
    )
    swap.start()

    together = 6

    def distances(step, carry):
        near_in = []
        for u in range(0, together, 2):
            sides = []
            for v in range(2):
                ry = step * together + u + v
                value = ytab[pl.ds(ry, 48, stride=48), :]
                sides.append(
                    jnp.concatenate([value.astype(BF), times_i(value).astype(BF)], axis=0)
                )
            out = dot(xf_ref[...], jnp.concatenate(sides, axis=1)).astype(BF)
            near_in += [out[:, :128], out[:, 128:]]
        near_in = jnp.concatenate(near_in, axis=0)
        near = dot(jnp.concatenate([near_in, near_in], axis=1), tb[...])
        far_parts = []
        for u in range(together):
            ry = step * together + u
            w_re = wre_full[pl.ds(ry, 48, stride=48), :]
            w_im = wim_full[pl.ds(ry, 48, stride=48), :]
            n_re, n_im = near[u * 48:u * 48 + 48, :128], near[u * 48:u * 48 + 48, 128:]
            far_re = -(n_re * w_im + n_im * w_re)
            far_im = n_re * w_re - n_im * w_im
            far_parts.append(jnp.concatenate([far_re.astype(BF), far_im.astype(BF)], axis=1))
        far = jnp.concatenate(far_parts, axis=0)
        home = dot(far, pb[0:256, :]) + dot(far, pb[256:512, :])
        for u in range(0, together, 2):
            sides = []
            for v in range(2):
                value = home[(u + v) * 48:(u + v) * 48 + 48, :]
                sides.append(
                    jnp.concatenate([value.astype(BF), times_i(value).astype(BF)], axis=0)
                )
            out = dot(xi_ref[...], jnp.concatenate(sides, axis=1))
            for v in range(2):
                at = pl.multiple_of((step * together + u + v) * 48, 8)
                utab[pl.ds(at, 48), :] = out[:, v * 128:v * 128 + 128]
        return carry

    lax.fori_loop(0, 48 // together, distances, 0)

    def send2(t, carry):
        grp = (mine + t) % 16
        value = jnp.concatenate(
            [utab[pl.ds(grp * 3 + u, 48, stride=48), :] for u in range(3)], axis=0
        )
        stacked = jnp.concatenate([value.astype(BF), times_i(value).astype(BF)], axis=0)
        out = dot(yi_ref[...], stacked)
        for i in range(4):
            v0 = out[i * 2 * PAD:i * 2 * PAD + PAD]
            v1 = out[i * 2 * PAD + PAD:i * 2 * PAD + 2 * PAD]
            first = jnp.where(low32, v0, pltpu.roll(v1, 32, 1))
            second = jnp.where(low32, pltpu.roll(v0, 96, 1), v1)
            packed2[grp, i] = first[:hk].astype(BF).reshape(hk // 2, 2, width)
            packed2[grp, 4 + i] = second[:hk].astype(BF).reshape(hk // 2, 2, width)
        for slot in range(8):
            @pl.when((t != 0) | (slot != place))
            def _():
                pltpu.make_async_remote_copy(
                    src_ref=packed2.at[grp, slot], dst_ref=landed2.at[mine, place],
                    send_sem=ssem2, recv_sem=rsem2.at[t],
                    device_id=device_of(grp, slot), device_id_type=MESH,
                ).start()
        return carry

    lax.fori_loop(0, 16, send2, 0)
    own2 = pltpu.make_async_copy(packed2.at[mine, place], landed2.at[mine, place], lsem)
    own2.start()

    swap.wait()
    mine_at = pl.multiple_of(half * rows_m, 32)
    other_at = pl.multiple_of((1 - half) * rows_m, 32)

    def build(k, carry):
        for ref, at in ((green_ref, mine_at), (partner, other_at)):
            value = ref[k]
            turned = (pltpu.roll(value.astype(F32), 64, 1) * -minus_low).astype(BF)
            gmat[k, pl.ds(at, rows_m), :] = turned
            gmat[k, pl.ds(64 + at, rows_m), :] = value
        return carry

    lax.fori_loop(0, count_k, build, 0)
    own2.wait()

    def arrive2(t, carry):
        grp = (mine + 16 - t) % 16

        @pl.when(t == 0)
        def _():
            ref = landed2.at[grp, pl.ds(0, 7)]
            pltpu.make_async_copy(ref, ref, rsem2.at[t]).wait()

        @pl.when(t != 0)
        def _():
            ref = landed2.at[grp]
            pltpu.make_async_copy(ref, ref, rsem2.at[t]).wait()

        for slot in range(8):
            value = landed2[grp, slot].reshape(hk, width).astype(F32)
            start = pl.multiple_of((grp * 8 + slot) * PAD, 8)
            pages[pl.ds(start, hk), :] = value
        return carry

    lax.fori_loop(0, 16, arrive2, 0)

    for r in range(hk):
        value = pages[pl.ds(r, 128, stride=PAD), :].T.astype(BF)
        for k2 in range(2):
            amat[(k2 * hk + r) * rows_m:(k2 * hk + r + 1) * rows_m, 0:128] = value[
                k2 * 32:k2 * 32 + 32
            ]
            amat[(k2 * hk + r) * rows_m:(k2 * hk + r + 1) * rows_m, 128:256] = value[
                64 + k2 * 32:64 + k2 * 32 + 32
            ]

    def coeffs(i, carry):
        at = pl.multiple_of(i * 192, 32)
        value = amat[pl.ds(at, 192), :]
        sigma = (dot(value, pq[0:256, :]) + dot(value, pq[256:512, :])).astype(BF)
        sigma_ref[pl.ds(i * 6, 6)] = sigma.reshape(6, rows_m, width)
        skm[pl.ds(at, 192), :] = dot(jnp.concatenate([sigma, sigma], axis=1), kb[...]).astype(BF)
        for u in range(6):
            k = i * 6 + u
            row = pl.multiple_of(i * 192 + u * 32, 32)
            memory = dot(skm[pl.ds(row, rows_m), :], gmat[k])
            turned = gmat[k, pl.ds(mine_at, rows_m), :].astype(F32)
            own = green_ref[k].astype(F32)
            energy = energy_ref[orbital, k]
            next_ref[k] = (own + STEP_SIZE * (energy * turned + memory)).astype(BF)
        return carry

    lax.fori_loop(0, count_k // 6, coeffs, 0)

    ref = landed1.at[pl.ds(0, 15)]
    pltpu.make_async_copy(ref, ref, ssem1).wait()
    ref = landed1.at[0, pl.ds(0, 7)]
    pltpu.make_async_copy(ref, ref, ssem1).wait()
    ref = landed2.at[pl.ds(0, 15)]
    pltpu.make_async_copy(ref, ref, ssem2).wait()
    ref = landed2.at[0, pl.ds(0, 7)]
    pltpu.make_async_copy(ref, ref, ssem2).wait()


def on_device(green_coeff, screened, band_energy, time_basis, projector, memory_kernel):
    total_k = screened.shape[0]
    tables = [jnp.asarray(t, BF) for t in phase_tables(48, green_coeff.shape[0], 4)]
    vmem = pl.BlockSpec(memory_space=pltpu.VMEM)
    dma = pltpu.SemaphoreType.DMA
    message = (16, 8, 9, 2, 128)
    out = pltpu.VMEM(green_coeff.shape, BF)
    return pl.pallas_call(
        kernel,
        out_shape=(out, out),
        in_specs=[pl.BlockSpec(memory_space=pl.ANY)] * 10,
        out_specs=(vmem, vmem),
        scratch_shapes=[
            pltpu.VMEM(green_coeff.shape, BF),
            pltpu.VMEM((total_k, 256), BF),
            pltpu.SMEM((2, green_coeff.shape[0]), F32),
            pltpu.VMEM(time_basis.shape, F32),
            pltpu.VMEM(time_basis.shape, F32),
            pltpu.VMEM(memory_kernel.shape, F32),
            *[pltpu.VMEM(t.shape, BF) for t in tables],
            dma((10,)),
            pltpu.VMEM((total_k, 128), F32),
            pltpu.VMEM((total_k, 128), F32),
            pltpu.VMEM((128 * PAD, 128), F32),
            pltpu.VMEM(message, BF),
            pltpu.VMEM(message, BF),
            pltpu.VMEM(message, BF),
            pltpu.VMEM(message, BF),
            pltpu.VMEM((total_k, 128), F32),
            pltpu.VMEM((total_k, 128), F32),
            pltpu.VMEM((8 * PAD, 128), F32),
            pltpu.VMEM((256, 256), BF),
            pltpu.VMEM((512, 128), BF),
            pltpu.VMEM((512, 128), BF),
            pltpu.VMEM((256, 128), BF),
            pltpu.VMEM((256, 128), F32),
            pltpu.VMEM(green_coeff.shape, BF),
            pltpu.VMEM((36, 128, 128), BF),
            pltpu.VMEM((1152, 256), BF),
            pltpu.VMEM((1152, 128), BF),
            dma, dma, dma((16,)), dma, dma((16,)), dma, dma,
        ],
        compiler_params=pltpu.CompilerParams(
            collective_id=0, has_side_effects=True, vmem_limit_bytes=60 * 2**20
        ),
    )(
        green_coeff,
        screened.reshape(total_k, 256),
        band_energy.T,
        time_basis,
        projector.T,
        memory_kernel,
        *tables,
    )


def solution(mesh):
    return jax.shard_map(
        on_device,
        mesh=mesh,
        in_specs=(P("ka", "ot", None), P(None, ("ot", "ka"), None), P("ka", None), P(), P(), P()),
        out_specs=(P("ka", "ot", None), P("ka", "ot", None)),
        check_vma=False,
    )
```

```python
import functools
import math

import jax
import jax.numpy as jnp
import numpy as np
from jax import lax
from jax.experimental import pallas as pl
from jax.experimental.pallas import tpu as pltpu
from jax.sharding import PartitionSpec as P

STEP_SIZE = 0.25
MESH = pl.DeviceIdType.MESH
BF = jnp.bfloat16
F32 = jnp.float32
PAD = 24


def phase_tables(lattice, block, group):
    kx_rows = group * block // lattice
    half = block // 2
    cosine = lambda a, b: np.cos(2.0 * math.pi * (a * b % lattice) / lattice)
    sine = lambda a, b: np.sin(2.0 * math.pi * (a * b % lattice) / lattice)
    idx = np.arange(lattice)
    cx, sx = cosine(idx[:, None], idx[None, :]), sine(idx[:, None], idx[None, :])
    x_fwd = np.concatenate([cx, sx], axis=1)
    x_inv = np.concatenate([cx, -sx], axis=1)
    row = np.arange(group * 2 * PAD)
    place, inner = row // PAD, row % PAD
    kk = (place // 2) * block + (place % 2) * half + inner
    valid = inner < half
    kx_of, ky_of = kk // lattice, kk % lattice
    lat_row = np.arange(kx_rows * lattice)
    rx_of, ry_of = lat_row // lattice, lat_row % lattice
    same = (rx_of[:, None] == kx_of[None, :]) & valid[None, :]
    cy = np.where(same, cosine(ry_of[:, None], ky_of[None, :]), 0.0)
    sy = np.where(same, sine(ry_of[:, None], ky_of[None, :]), 0.0)
    y_fwd = np.concatenate([cy, sy], axis=1)
    y_inv = np.concatenate([cy.T, -sy.T], axis=1)
    return [t.astype(np.float32) for t in (x_fwd, x_inv, y_fwd, y_inv)]


def split(value):
    high = value.astype(BF)
    return high, (value - high.astype(F32)).astype(BF)


def dot(left, right):
    return jnp.dot(left, right, preferred_element_type=F32)


def kernel(
    green_in, screen_in, energy_in, basis_in, proj_in, memk_in, xf_in, xi_in, yf_in, yi_in,
    sigma_ref, next_ref,
    green_ref, w_raw, energy_ref, basis_ref, proj_ref, memk_ref, xf_ref, xi_ref, yf_ref, yi_ref,
    fsem, plane_in, wre_full, wim_full, pages, packed1, landed1, packed2, landed2, ytab, utab, xbuf,
    tb, pb, pq, kb, pt, partner, gmat, amat, skm,
    lsem, ssem1, rsem1, ssem2, rsem2, psem, qsem,
):
    ka, ot = lax.axis_index("ka"), lax.axis_index("ot")
    half, orbital = ot % 2, ot // 2
    mine, place = ka // 4, half * 4 + ka % 4
    count_k, rows_m, width = green_ref.shape
    hk = count_k // 2

    def device_of(grp, slot):
        return (grp * 4 + slot % 4, orbital * 2 + slot // 4)

    barrier = pltpu.get_barrier_semaphore()

    def tell(semaphore, grp, slot):
        pl.semaphore_signal(semaphore, inc=1, device_id=device_of(grp, slot), device_id_type=MESH)

    fetches = [
        pltpu.make_async_copy(source, target, fsem.at[i])
        for i, (source, target) in enumerate([
            (green_in, green_ref), (basis_in, basis_ref), (screen_in, w_raw),
            (energy_in, energy_ref), (proj_in, proj_ref), (memk_in, memk_ref),
            (xf_in, xf_ref), (xi_in, xi_ref), (yf_in, yf_ref), (yi_in, yi_ref),
        ])
    ]
    for fetch in fetches:
        fetch.start()
    for s in range(1, 16):
        tell(barrier, mine ^ s, place)
    for s in range(1, 8):
        tell(barrier, mine, place ^ s)
    pl.semaphore_wait(barrier, 22)
    for s in range(1, 8):
        tell(plane_in, mine, place ^ s)
    for fetch in fetches[:2]:
        fetch.wait()


    def swap(part):
        lo, hi = ((0, 18), (18, count_k))[part]
        return pltpu.make_async_remote_copy(
            src_ref=green_ref.at[pl.ds(lo, hi - lo)], dst_ref=partner.at[pl.ds(lo, hi - lo)],
            send_sem=psem.at[part], recv_sem=qsem.at[part],
            device_id=(ka, orbital * 2 + 1 - half), device_id_type=MESH,
        )

    swap(0).start()

    lane64 = lax.broadcasted_iota(jnp.int32, (1, width), 1)
    low64 = lane64 < 64
    low32 = lane64 % 64 < 32
    minus_low = jnp.where(low64, -1.0, 1.0).astype(F32)

    def times_i(value):
        return pltpu.roll(value, 64, 1) * minus_low

    basis_t = basis_ref[...].T
    t_high, t_low = split(basis_t)
    t_cat = jnp.concatenate([t_high, t_low], axis=1)

    def rows_step(r, carry):
        parts = []
        both = [green_ref[r].astype(F32), green_ref[hk + r].astype(F32)]
        turned = [pltpu.roll(v, 64, 1) for v in both]
        for v, u in zip(both, turned):
            parts.append(jnp.where(low64, v, u))
        for v, u in zip(both, turned):
            parts.append(jnp.where(low64, u, v))
        right = jnp.concatenate(parts, axis=0).astype(BF)
        out = lax.dot_general(
            t_cat, right, (((1,), (1,)), ((), ())), preferred_element_type=F32
        )
        pages[pl.ds(r, 128, stride=PAD), :] = out
        return carry

    for r in range(hk):
        rows_step(r, 0)

    pl.semaphore_wait(plane_in, 7)

    def send1(t, carry):
        grp = (mine + t) % 16
        for slot in range(8):
            q = (slot // 4) * 64 + grp * 4 + slot % 4
            start = pl.multiple_of(q * PAD, 8)
            value = pages[pl.ds(start, hk), :].astype(BF)
            packed1[grp, slot] = value.reshape(hk // 2, 2, width)
        for slot in range(8):
            @pl.when((t != 0) | (slot != place))
            def _():
                pltpu.make_async_remote_copy(
                    src_ref=packed1.at[grp, slot], dst_ref=landed1.at[mine, place],
                    send_sem=ssem1, recv_sem=rsem1.at[t],
                    device_id=device_of(grp, slot), device_id_type=MESH,
                ).start()
        return carry

    lax.fori_loop(0, 16, send1, 0)
    own1 = pltpu.make_async_copy(packed1.at[mine, place], landed1.at[mine, place], lsem)
    own1.start()

    for fetch in fetches[2:]:
        fetch.wait()
    zeros = jnp.zeros((64, 128), F32)
    basis = basis_ref[...]
    wide = jnp.concatenate(
        [jnp.concatenate([basis, zeros], axis=1), jnp.concatenate([zeros, basis], axis=1)], axis=0
    )
    high, low = split(wide)
    tb[0:128, :] = high
    tb[128:256, :] = low
    proj = proj_ref[...].T
    blank = jnp.zeros((128, 64), F32)
    left, right = jnp.concatenate([proj, blank], axis=1), jnp.concatenate([blank, proj], axis=1)
    for offset, piece in ((0, left), (128, right)):
        high, low = split(piece)
        pb[offset:offset + 128, :] = high
        pb[256 + offset:256 + offset + 128, :] = low
    pt[0:128, :] = left
    for grp in range(16):
        for h in range(2):
            pt[pl.ds(128 + grp * 8 + h * 4, 4), :] = pt[pl.ds(h * 64 + grp * 4, 4), :]
    left = pt[128:256, :]
    right = pltpu.roll(left, 64, 1)
    for offset, piece in ((0, left), (128, right)):
        high, low = split(piece)
        pq[offset:offset + 128, :] = high
        pq[256 + offset:256 + offset + 128, :] = low
    memk = memk_ref[...]
    blank = jnp.zeros((64, 64), F32)
    wide = jnp.concatenate(
        [jnp.concatenate([memk, blank], axis=1), jnp.concatenate([blank, memk], axis=1)], axis=0
    )
    high, low = split(wide)
    kb[0:128, :] = high
    kb[128:256, :] = low
    scale = 1.0 / w_raw.shape[0]

    def widen(i, carry):
        value = w_raw[pl.ds(pl.multiple_of(i * 48, 16), 48), :].astype(F32) * scale
        wre_full[pl.ds(i, 48, stride=48), :] = value[:, :128]
        wim_full[pl.ds(i, 48, stride=48), :] = value[:, 128:]
        return carry

    lax.fori_loop(0, 48, widen, 0)
    xbuf[...] = jnp.zeros_like(xbuf)
    own1.wait()

    def arrive1(t, carry):
        grp = (mine + 16 - t) % 16

        @pl.when(t == 0)
        def _():
            ref = landed1.at[grp, pl.ds(0, 7)]
            pltpu.make_async_copy(ref, ref, rsem1.at[t]).wait()

        @pl.when(t != 0)
        def _():
            ref = landed1.at[grp]
            pltpu.make_async_copy(ref, ref, rsem1.at[t]).wait()

        for i in range(4):
            v0 = landed1[grp, i].reshape(hk, width).astype(F32)
            v1 = landed1[grp, 4 + i].reshape(hk, width).astype(F32)
            xbuf[i * 2 * PAD:i * 2 * PAD + hk, :] = jnp.where(low32, v0, pltpu.roll(v1, 32, 1))
            xbuf[i * 2 * PAD + PAD:i * 2 * PAD + PAD + hk, :] = jnp.where(
                low32, pltpu.roll(v0, 96, 1), v1
            )
        value = xbuf[...]
        stacked = jnp.concatenate([value.astype(BF), times_i(value).astype(BF)], axis=0)
        out = dot(yf_ref[...], stacked)
        for u in range(3):
            ytab[pl.ds(grp * 3 + u, 48, stride=48), :] = out[u * 48:u * 48 + 48]
        return carry

    lax.fori_loop(0, 16, arrive1, 0)

    swap(1).start()

    together = 12

    def distances(step, carry):
        near_in = []
        for u in range(0, together, 2):
            sides = []
            for v in range(2):
                ry = step * together + u + v
                value = ytab[pl.ds(pl.multiple_of(ry * 48, 8), 48), :]
                sides.append(
                    jnp.concatenate([value.astype(BF), times_i(value).astype(BF)], axis=0)
                )
            out = dot(xf_ref[...], jnp.concatenate(sides, axis=1)).astype(BF)
            near_in += [out[:, :128], out[:, 128:]]
        near_in = jnp.concatenate(near_in, axis=0)
        near = dot(jnp.concatenate([near_in, near_in], axis=1), tb[...])
        far_parts = []
        for u in range(together):
            ry = step * together + u
            w_re = wre_full[pl.ds(pl.multiple_of(ry * 48, 8), 48), :]
            w_im = wim_full[pl.ds(pl.multiple_of(ry * 48, 8), 48), :]
            n_re, n_im = near[u * 48:u * 48 + 48, :128], near[u * 48:u * 48 + 48, 128:]
            far_re = -(n_re * w_im + n_im * w_re)
            far_im = n_re * w_re - n_im * w_im
            far_parts.append(jnp.concatenate([far_re.astype(BF), far_im.astype(BF)], axis=1))
        far = jnp.concatenate(far_parts, axis=0)
        home = dot(far, pb[0:256, :]) + dot(far, pb[256:512, :])
        for u in range(0, together, 2):
            sides = []
            for v in range(2):
                value = home[(u + v) * 48:(u + v) * 48 + 48, :]
                sides.append(
                    jnp.concatenate([value.astype(BF), times_i(value).astype(BF)], axis=0)
                )
            out = dot(xi_ref[...], jnp.concatenate(sides, axis=1))
            for v in range(2):
                at = pl.multiple_of((step * together + u + v) * 48, 8)
                utab[pl.ds(at, 48), :] = out[:, v * 128:v * 128 + 128]
        return carry

    lax.fori_loop(0, 48 // together, distances, 0)

    def send2(t, carry):
        grp = (mine + t) % 16
        value = jnp.concatenate(
            [utab[pl.ds(grp * 3 + u, 48, stride=48), :] for u in range(3)], axis=0
        )
        stacked = jnp.concatenate([value.astype(BF), times_i(value).astype(BF)], axis=0)
        out = dot(yi_ref[...], stacked)
        for i in range(4):
            v0 = out[i * 2 * PAD:i * 2 * PAD + PAD]
            v1 = out[i * 2 * PAD + PAD:i * 2 * PAD + 2 * PAD]
            first = jnp.where(low32, v0, pltpu.roll(v1, 32, 1))
            second = jnp.where(low32, pltpu.roll(v0, 96, 1), v1)
            packed2[grp, i] = first[:hk].astype(BF).reshape(hk // 2, 2, width)
            packed2[grp, 4 + i] = second[:hk].astype(BF).reshape(hk // 2, 2, width)
        for slot in range(8):
            @pl.when((t != 0) | (slot != place))
            def _():
                pltpu.make_async_remote_copy(
                    src_ref=packed2.at[grp, slot], dst_ref=landed2.at[mine, place],
                    send_sem=ssem2, recv_sem=rsem2.at[t],
                    device_id=device_of(grp, slot), device_id_type=MESH,
                ).start()
        return carry

    lax.fori_loop(0, 16, send2, 0)
    own2 = pltpu.make_async_copy(packed2.at[mine, place], landed2.at[mine, place], lsem)
    own2.start()

    swap(0).wait()
    swap(1).wait()
    mine_at = pl.multiple_of(half * rows_m, 32)
    other_at = pl.multiple_of((1 - half) * rows_m, 32)

    def build(k, carry):
        for ref, at in ((green_ref, mine_at), (partner, other_at)):
            value = ref[k]
            turned = (pltpu.roll(value.astype(F32), 64, 1) * -minus_low).astype(BF)
            gmat[k, pl.ds(at, rows_m), :] = turned
            gmat[k, pl.ds(64 + at, rows_m), :] = value
        return carry

    lax.fori_loop(0, count_k, build, 0)
    own2.wait()

    def arrive2(t, carry):
        grp = (mine + 16 - t) % 16

        @pl.when(t == 0)
        def _():
            ref = landed2.at[grp, pl.ds(0, 7)]
            pltpu.make_async_copy(ref, ref, rsem2.at[t]).wait()

        @pl.when(t != 0)
        def _():
            ref = landed2.at[grp]
            pltpu.make_async_copy(ref, ref, rsem2.at[t]).wait()

        for slot in range(8):
            value = landed2[grp, slot].reshape(hk, width).astype(F32)
            start = pl.multiple_of((grp * 8 + slot) * PAD, 8)
            pages[pl.ds(start, hk), :] = value
        return carry

    lax.fori_loop(0, 16, arrive2, 0)

    for r in range(hk):
        value = pages[pl.ds(r, 128, stride=PAD), :].T.astype(BF)
        for k2 in range(2):
            amat[(k2 * hk + r) * rows_m:(k2 * hk + r + 1) * rows_m, 0:128] = value[
                k2 * 32:k2 * 32 + 32
            ]
            amat[(k2 * hk + r) * rows_m:(k2 * hk + r + 1) * rows_m, 128:256] = value[
                64 + k2 * 32:64 + k2 * 32 + 32
            ]

    def coeffs(i, carry):
        at = pl.multiple_of(i * 384, 32)
        value = amat[pl.ds(at, 384), :]
        sigma = (dot(value, pq[0:256, :]) + dot(value, pq[256:512, :])).astype(BF)
        sigma_ref[pl.ds(i * 12, 12)] = sigma.reshape(12, rows_m, width)
        skm[pl.ds(at, 384), :] = dot(jnp.concatenate([sigma, sigma], axis=1), kb[...]).astype(BF)
        for u in range(12):
            k = i * 12 + u
            row = pl.multiple_of(i * 384 + u * 32, 32)
            memory = dot(skm[pl.ds(row, rows_m), :], gmat[k])
            turned = gmat[k, pl.ds(mine_at, rows_m), :].astype(F32)
            own = green_ref[k].astype(F32)
            energy = energy_ref[orbital, k]
            next_ref[k] = (own + STEP_SIZE * (energy * turned + memory)).astype(BF)
        return carry

    lax.fori_loop(0, count_k // 12, coeffs, 0)

    ref = landed1.at[pl.ds(0, 15)]
    pltpu.make_async_copy(ref, ref, ssem1).wait()
    ref = landed1.at[0, pl.ds(0, 7)]
    pltpu.make_async_copy(ref, ref, ssem1).wait()
    ref = landed2.at[pl.ds(0, 15)]
    pltpu.make_async_copy(ref, ref, ssem2).wait()
    ref = landed2.at[0, pl.ds(0, 7)]
    pltpu.make_async_copy(ref, ref, ssem2).wait()


def on_device(green_coeff, screened, band_energy, time_basis, projector, memory_kernel):
    total_k = screened.shape[0]
    tables = [jnp.asarray(t, BF) for t in phase_tables(48, green_coeff.shape[0], 4)]
    vmem = pl.BlockSpec(memory_space=pltpu.VMEM)
    dma = pltpu.SemaphoreType.DMA
    message = (16, 8, 9, 2, 128)
    out = pltpu.VMEM(green_coeff.shape, BF)
    return pl.pallas_call(
        kernel,
        out_shape=(out, out),
        in_specs=[pl.BlockSpec(memory_space=pl.ANY)] * 10,
        out_specs=(vmem, vmem),
        scratch_shapes=[
            pltpu.VMEM(green_coeff.shape, BF),
            pltpu.VMEM((total_k, 256), BF),
            pltpu.SMEM((2, green_coeff.shape[0]), F32),
            pltpu.VMEM(time_basis.shape, F32),
            pltpu.VMEM(time_basis.shape, F32),
            pltpu.VMEM(memory_kernel.shape, F32),
            *[pltpu.VMEM(t.shape, BF) for t in tables],
            dma((10,)),
            pltpu.SemaphoreType.REGULAR,
            pltpu.VMEM((total_k, 128), F32),
            pltpu.VMEM((total_k, 128), F32),
            pltpu.VMEM((128 * PAD, 128), F32),
            pltpu.VMEM(message, BF),
            pltpu.VMEM(message, BF),
            pltpu.VMEM(message, BF),
            pltpu.VMEM(message, BF),
            pltpu.VMEM((total_k, 128), F32),
            pltpu.VMEM((total_k, 128), F32),
            pltpu.VMEM((8 * PAD, 128), F32),
            pltpu.VMEM((256, 256), BF),
            pltpu.VMEM((512, 128), BF),
            pltpu.VMEM((512, 128), BF),
            pltpu.VMEM((256, 128), BF),
            pltpu.VMEM((256, 128), F32),
            pltpu.VMEM(green_coeff.shape, BF),
            pltpu.VMEM((36, 128, 128), BF),
            pltpu.VMEM((1152, 256), BF),
            pltpu.VMEM((1152, 128), BF),
            dma, dma, dma((16,)), dma, dma((16,)), dma((2,)), dma((2,)),
        ],
        compiler_params=pltpu.CompilerParams(
            collective_id=0, has_side_effects=True, vmem_limit_bytes=60 * 2**20
        ),
    )(
        green_coeff,
        screened.reshape(total_k, 256),
        band_energy.T,
        time_basis,
        projector.T,
        memory_kernel,
        *tables,
    )


def solution(mesh):
    return jax.shard_map(
        on_device,
        mesh=mesh,
        in_specs=(P("ka", "ot", None), P(None, ("ot", "ka"), None), P("ka", None), P(), P(), P()),
        out_specs=(P("ka", "ot", None), P("ka", "ot", None)),
        check_vma=False,
    )
```

```python
import functools
import math

import jax
import jax.numpy as jnp
import numpy as np
from jax import lax
from jax.experimental import pallas as pl
from jax.experimental.pallas import tpu as pltpu
from jax.sharding import PartitionSpec as P

STEP_SIZE = 0.25
MESH = pl.DeviceIdType.MESH
BF = jnp.bfloat16
F32 = jnp.float32
PAD = 24


def phase_tables(lattice, block, group):
    kx_rows = group * block // lattice
    half = block // 2
    cosine = lambda a, b: np.cos(2.0 * math.pi * (a * b % lattice) / lattice)
    sine = lambda a, b: np.sin(2.0 * math.pi * (a * b % lattice) / lattice)
    idx = np.arange(lattice)
    cx, sx = cosine(idx[:, None], idx[None, :]), sine(idx[:, None], idx[None, :])
    x_fwd = np.kron(np.eye(3), np.concatenate([cx, sx], axis=0))
    x_inv = np.concatenate([cx, -sx], axis=1)
    row = np.arange(group * 2 * PAD)
    place, inner = row // PAD, row % PAD
    kk = (place // 2) * block + (place % 2) * half + inner
    valid = inner < half
    kx_of, ky_of = kk // lattice, kk % lattice
    lat_row = np.arange(kx_rows * lattice)
    rx_of, ry_of = lat_row // lattice, lat_row % lattice
    same = (rx_of[:, None] == kx_of[None, :]) & valid[None, :]
    cy = np.where(same, cosine(ry_of[:, None], ky_of[None, :]), 0.0)
    sy = np.where(same, sine(ry_of[:, None], ky_of[None, :]), 0.0)
    y_fwd = np.concatenate([cy, sy], axis=1)
    y_inv = np.concatenate([cy.T, -sy.T], axis=1)
    return [t.astype(np.float32) for t in (x_fwd, x_inv, y_fwd, y_inv)]


def split(value):
    high = value.astype(BF)
    return high, (value - high.astype(F32)).astype(BF)


def dot(left, right):
    return jnp.dot(left, right, preferred_element_type=F32)


def kernel(
    green_in, screen_in, energy_in, basis_in, proj_in, memk_in, xf_in, xi_in, yf_in, yi_in,
    sigma_ref, next_ref,
    green_ref, w_raw, energy_ref, basis_ref, proj_ref, memk_ref, xf_ref, xi_ref, yf_ref, yi_ref,
    fsem, plane_in, wre_full, wim_full, pages, packed1, landed1, packed2, landed2, ytab, utab, xbuf,
    tb, pb, pq, kb, pt, partner, gmat, amat, skm,
    lsem, ssem1, rsem1, ssem2, rsem2, psem, qsem,
):
    ka, ot = lax.axis_index("ka"), lax.axis_index("ot")
    half, orbital = ot % 2, ot // 2
    mine, place = ka // 4, half * 4 + ka % 4
    count_k, rows_m, width = green_ref.shape
    hk = count_k // 2

    def device_of(grp, slot):
        return (grp * 4 + slot % 4, orbital * 2 + slot // 4)

    barrier = pltpu.get_barrier_semaphore()

    def tell(semaphore, grp, slot):
        pl.semaphore_signal(semaphore, inc=1, device_id=device_of(grp, slot), device_id_type=MESH)

    fetches = [
        pltpu.make_async_copy(source, target, fsem.at[i])
        for i, (source, target) in enumerate([
            (green_in, green_ref), (basis_in, basis_ref), (screen_in, w_raw),
            (energy_in, energy_ref), (proj_in, proj_ref), (memk_in, memk_ref),
            (xf_in, xf_ref), (xi_in, xi_ref), (yf_in, yf_ref), (yi_in, yi_ref),
        ])
    ]
    for fetch in fetches:
        fetch.start()
    for s in range(1, 16):
        tell(barrier, mine ^ s, place)
    for s in range(1, 8):
        tell(barrier, mine, place ^ s)
    pl.semaphore_wait(barrier, 22)
    for s in range(1, 8):
        tell(plane_in, mine, place ^ s)
    for fetch in fetches[:2]:
        fetch.wait()


    def swap(part):
        lo, hi = ((0, 18), (18, count_k))[part]
        return pltpu.make_async_remote_copy(
            src_ref=green_ref.at[pl.ds(lo, hi - lo)], dst_ref=partner.at[pl.ds(lo, hi - lo)],
            send_sem=psem.at[part], recv_sem=qsem.at[part],
            device_id=(ka, orbital * 2 + 1 - half), device_id_type=MESH,
        )

    swap(0).start()

    lane64 = lax.broadcasted_iota(jnp.int32, (1, width), 1)
    low64 = lane64 < 64
    low32 = lane64 % 64 < 32
    minus_low = jnp.where(low64, -1.0, 1.0).astype(F32)

    def times_i(value):
        return pltpu.roll(value, 64, 1) * minus_low

    basis_t = basis_ref[...].T
    t_high, t_low = split(basis_t)
    t_cat = jnp.concatenate([t_high, t_low], axis=1)

    def rows_step(r, carry):
        parts = []
        both = [green_ref[r].astype(F32), green_ref[hk + r].astype(F32)]
        turned = [pltpu.roll(v, 64, 1) for v in both]
        for v, u in zip(both, turned):
            parts.append(jnp.where(low64, v, u))
        for v, u in zip(both, turned):
            parts.append(jnp.where(low64, u, v))
        right = jnp.concatenate(parts, axis=0).astype(BF)
        out = lax.dot_general(
            t_cat, right, (((1,), (1,)), ((), ())), preferred_element_type=F32
        )
        pages[pl.ds(r, 128, stride=PAD), :] = out
        return carry

    for r in range(hk):
        rows_step(r, 0)

    pl.semaphore_wait(plane_in, 7)

    def send1(t, carry):
        grp = (mine + t) % 16
        for slot in range(8):
            q = (slot // 4) * 64 + grp * 4 + slot % 4
            start = pl.multiple_of(q * PAD, 8)
            value = pages[pl.ds(start, hk), :].astype(BF)
            packed1[grp, slot] = value.reshape(hk // 2, 2, width)
        for slot in range(8):
            @pl.when((t != 0) | (slot != place))
            def _():
                pltpu.make_async_remote_copy(
                    src_ref=packed1.at[grp, slot], dst_ref=landed1.at[mine, place],
                    send_sem=ssem1, recv_sem=rsem1.at[t],
                    device_id=device_of(grp, slot), device_id_type=MESH,
                ).start()
        return carry

    lax.fori_loop(0, 16, send1, 0)
    own1 = pltpu.make_async_copy(packed1.at[mine, place], landed1.at[mine, place], lsem)
    own1.start()

    for fetch in fetches[2:]:
        fetch.wait()
    zeros = jnp.zeros((64, 128), F32)
    basis = basis_ref[...]
    wide = jnp.concatenate(
        [jnp.concatenate([basis, zeros], axis=1), jnp.concatenate([zeros, basis], axis=1)], axis=0
    )
    high, low = split(wide)
    tb[0:128, :] = high
    tb[128:256, :] = low
    proj = proj_ref[...].T
    blank = jnp.zeros((128, 64), F32)
    left, right = jnp.concatenate([proj, blank], axis=1), jnp.concatenate([blank, proj], axis=1)
    for offset, piece in ((0, left), (128, right)):
        high, low = split(piece)
        pb[offset:offset + 128, :] = high
        pb[256 + offset:256 + offset + 128, :] = low
    pt[0:128, :] = left
    for grp in range(16):
        for h in range(2):
            pt[pl.ds(128 + grp * 8 + h * 4, 4), :] = pt[pl.ds(h * 64 + grp * 4, 4), :]
    left = pt[128:256, :]
    right = pltpu.roll(left, 64, 1)
    for offset, piece in ((0, left), (128, right)):
        high, low = split(piece)
        pq[offset:offset + 128, :] = high
        pq[256 + offset:256 + offset + 128, :] = low
    memk = memk_ref[...]
    blank = jnp.zeros((64, 64), F32)
    wide = jnp.concatenate(
        [jnp.concatenate([memk, blank], axis=1), jnp.concatenate([blank, memk], axis=1)], axis=0
    )
    high, low = split(wide)
    kb[0:128, :] = high
    kb[128:256, :] = low
    scale = 1.0 / w_raw.shape[0]

    def widen(i, carry):
        value = w_raw[pl.ds(pl.multiple_of(i * 48, 16), 48), :].astype(F32) * scale
        wre_full[pl.ds(i, 48, stride=48), :] = value[:, :128]
        wim_full[pl.ds(i, 48, stride=48), :] = value[:, 128:]
        return carry

    lax.fori_loop(0, 48, widen, 0)
    xbuf[...] = jnp.zeros_like(xbuf)
    own1.wait()

    def arrive1(t, carry):
        grp = (mine + 16 - t) % 16

        @pl.when(t == 0)
        def _():
            ref = landed1.at[grp, pl.ds(0, 7)]
            pltpu.make_async_copy(ref, ref, rsem1.at[t]).wait()

        @pl.when(t != 0)
        def _():
            ref = landed1.at[grp]
            pltpu.make_async_copy(ref, ref, rsem1.at[t]).wait()

        for i in range(4):
            v0 = landed1[grp, i].reshape(hk, width).astype(F32)
            v1 = landed1[grp, 4 + i].reshape(hk, width).astype(F32)
            xbuf[i * 2 * PAD:i * 2 * PAD + hk, :] = jnp.where(low32, v0, pltpu.roll(v1, 32, 1))
            xbuf[i * 2 * PAD + PAD:i * 2 * PAD + PAD + hk, :] = jnp.where(
                low32, pltpu.roll(v0, 96, 1), v1
            )
        value = xbuf[...]
        stacked = jnp.concatenate([value.astype(BF), times_i(value).astype(BF)], axis=0)
        out = dot(yf_ref[...], stacked)
        for u in range(3):
            ytab[pl.ds(grp * 3 + u, 48, stride=48), :] = out[u * 48:u * 48 + 48]
        return carry

    lax.fori_loop(0, 16, arrive1, 0)

    swap(1).start()

    together = 24

    def along_x(values, sign):
        done = []
        for u in range(0, len(values), 2 * 3):
            sides = [
                jnp.concatenate([v.astype(BF) for v in values[at:at + 3]], axis=0)
                for at in (u, u + 3)
            ]
            out = dot(xf_ref[...], jnp.concatenate(sides, axis=1))
            for v in range(2):
                for at in range(0, 96 * 3, 96):
                    even = out[at:at + 48, v * 128:v * 128 + 128]
                    odd = out[at + 48:at + 96, v * 128:v * 128 + 128]
                    done.append(even + pltpu.roll(odd, 64, 1) * (minus_low * sign))
        return done


    def distances(step, carry):
        near_in = along_x(
            [ytab[pl.ds(pl.multiple_of((step * together + u) * 48, 8), 48), :] for u in range(together)],
            1.0,
        )
        near_in = [v.astype(BF) for v in near_in]
        near_in = jnp.concatenate(near_in, axis=0)
        near = dot(jnp.concatenate([near_in, near_in], axis=1), tb[...])
        far_parts = []
        for u in range(together):
            ry = step * together + u
            w_re = wre_full[pl.ds(pl.multiple_of(ry * 48, 8), 48), :]
            w_im = wim_full[pl.ds(pl.multiple_of(ry * 48, 8), 48), :]
            n_re, n_im = near[u * 48:u * 48 + 48, :128], near[u * 48:u * 48 + 48, 128:]
            far_re = -(n_re * w_im + n_im * w_re)
            far_im = n_re * w_re - n_im * w_im
            far_parts.append(jnp.concatenate([far_re.astype(BF), far_im.astype(BF)], axis=1))
        far = jnp.concatenate(far_parts, axis=0)
        home = dot(far, pb[0:256, :]) + dot(far, pb[256:512, :])
        back = along_x([home[u * 48:u * 48 + 48, :] for u in range(together)], -1.0)
        for u in range(together):
            utab[pl.ds(pl.multiple_of((step * together + u) * 48, 8), 48), :] = back[u]
        return carry

    lax.fori_loop(0, 48 // together, distances, 0)

    def send2(t, carry):
        grp = (mine + t) % 16
        value = jnp.concatenate(
            [utab[pl.ds(grp * 3 + u, 48, stride=48), :] for u in range(3)], axis=0
        )
        stacked = jnp.concatenate([value.astype(BF), times_i(value).astype(BF)], axis=0)
        out = dot(yi_ref[...], stacked)
        for i in range(4):
            v0 = out[i * 2 * PAD:i * 2 * PAD + PAD]
            v1 = out[i * 2 * PAD + PAD:i * 2 * PAD + 2 * PAD]
            first = jnp.where(low32, v0, pltpu.roll(v1, 32, 1))
            second = jnp.where(low32, pltpu.roll(v0, 96, 1), v1)
            packed2[grp, i] = first[:hk].astype(BF).reshape(hk // 2, 2, width)
            packed2[grp, 4 + i] = second[:hk].astype(BF).reshape(hk // 2, 2, width)
        for slot in range(8):
            @pl.when((t != 0) | (slot != place))
            def _():
                pltpu.make_async_remote_copy(
                    src_ref=packed2.at[grp, slot], dst_ref=landed2.at[mine, place],
                    send_sem=ssem2, recv_sem=rsem2.at[t],
                    device_id=device_of(grp, slot), device_id_type=MESH,
                ).start()
        return carry

    lax.fori_loop(0, 16, send2, 0)
    own2 = pltpu.make_async_copy(packed2.at[mine, place], landed2.at[mine, place], lsem)
    own2.start()

    swap(0).wait()
    swap(1).wait()
    mine_at = pl.multiple_of(half * rows_m, 32)
    other_at = pl.multiple_of((1 - half) * rows_m, 32)

    def build(k, carry):
        for ref, at in ((green_ref, mine_at), (partner, other_at)):
            value = ref[k]
            turned = (pltpu.roll(value.astype(F32), 64, 1) * -minus_low).astype(BF)
            gmat[k, pl.ds(at, rows_m), :] = turned
            gmat[k, pl.ds(64 + at, rows_m), :] = value
        return carry

    lax.fori_loop(0, count_k, build, 0)
    own2.wait()

    def arrive2(t, carry):
        grp = (mine + 16 - t) % 16

        @pl.when(t == 0)
        def _():
            ref = landed2.at[grp, pl.ds(0, 7)]
            pltpu.make_async_copy(ref, ref, rsem2.at[t]).wait()

        @pl.when(t != 0)
        def _():
            ref = landed2.at[grp]
            pltpu.make_async_copy(ref, ref, rsem2.at[t]).wait()

        for slot in range(8):
            value = landed2[grp, slot].reshape(hk, width).astype(F32)
            start = pl.multiple_of((grp * 8 + slot) * PAD, 8)
            pages[pl.ds(start, hk), :] = value
        return carry

    lax.fori_loop(0, 16, arrive2, 0)

    for r in range(hk):
        value = pages[pl.ds(r, 128, stride=PAD), :].T.astype(BF)
        for k2 in range(2):
            amat[(k2 * hk + r) * rows_m:(k2 * hk + r + 1) * rows_m, 0:128] = value[
                k2 * 32:k2 * 32 + 32
            ]
            amat[(k2 * hk + r) * rows_m:(k2 * hk + r + 1) * rows_m, 128:256] = value[
                64 + k2 * 32:64 + k2 * 32 + 32
            ]

    def coeffs(i, carry):
        at = pl.multiple_of(i * 1152, 32)
        value = amat[pl.ds(at, 1152), :]
        sigma = (dot(value, pq[0:256, :]) + dot(value, pq[256:512, :])).astype(BF)
        sigma_ref[pl.ds(i * 36, 36)] = sigma.reshape(36, rows_m, width)
        skm[pl.ds(at, 1152), :] = dot(jnp.concatenate([sigma, sigma], axis=1), kb[...]).astype(BF)
        for u in range(36):
            k = i * 36 + u
            row = pl.multiple_of(i * 1152 + u * 32, 32)
            memory = dot(skm[pl.ds(row, rows_m), :], gmat[k])
            turned = gmat[k, pl.ds(mine_at, rows_m), :].astype(F32)
            own = green_ref[k].astype(F32)
            energy = energy_ref[orbital, k]
            next_ref[k] = (own + STEP_SIZE * (energy * turned + memory)).astype(BF)
        return carry

    lax.fori_loop(0, count_k // 36, coeffs, 0)

    ref = landed1.at[pl.ds(0, 15)]
    pltpu.make_async_copy(ref, ref, ssem1).wait()
    ref = landed1.at[0, pl.ds(0, 7)]
    pltpu.make_async_copy(ref, ref, ssem1).wait()
    ref = landed2.at[pl.ds(0, 15)]
    pltpu.make_async_copy(ref, ref, ssem2).wait()
    ref = landed2.at[0, pl.ds(0, 7)]
    pltpu.make_async_copy(ref, ref, ssem2).wait()


def on_device(green_coeff, screened, band_energy, time_basis, projector, memory_kernel):
    total_k = screened.shape[0]
    tables = [jnp.asarray(t, BF) for t in phase_tables(48, green_coeff.shape[0], 4)]
    vmem = pl.BlockSpec(memory_space=pltpu.VMEM)
    dma = pltpu.SemaphoreType.DMA
    message = (16, 8, 9, 2, 128)
    out = pltpu.VMEM(green_coeff.shape, BF)
    return pl.pallas_call(
        kernel,
        out_shape=(out, out),
        in_specs=[pl.BlockSpec(memory_space=pl.ANY)] * 10,
        out_specs=(vmem, vmem),
        scratch_shapes=[
            pltpu.VMEM(green_coeff.shape, BF),
            pltpu.VMEM((total_k, 256), BF),
            pltpu.SMEM((2, green_coeff.shape[0]), F32),
            pltpu.VMEM(time_basis.shape, F32),
            pltpu.VMEM(time_basis.shape, F32),
            pltpu.VMEM(memory_kernel.shape, F32),
            *[pltpu.VMEM(t.shape, BF) for t in tables],
            dma((10,)),
            pltpu.SemaphoreType.REGULAR,
            pltpu.VMEM((total_k, 128), F32),
            pltpu.VMEM((total_k, 128), F32),
            pltpu.VMEM((128 * PAD, 128), F32),
            pltpu.VMEM(message, BF),
            pltpu.VMEM(message, BF),
            pltpu.VMEM(message, BF),
            pltpu.VMEM(message, BF),
            pltpu.VMEM((total_k, 128), F32),
            pltpu.VMEM((total_k, 128), F32),
            pltpu.VMEM((8 * PAD, 128), F32),
            pltpu.VMEM((256, 256), BF),
            pltpu.VMEM((512, 128), BF),
            pltpu.VMEM((512, 128), BF),
            pltpu.VMEM((256, 128), BF),
            pltpu.VMEM((256, 128), F32),
            pltpu.VMEM(green_coeff.shape, BF),
            pltpu.VMEM((36, 128, 128), BF),
            pltpu.VMEM((1152, 256), BF),
            pltpu.VMEM((1152, 128), BF),
            dma, dma, dma((16,)), dma, dma((16,)), dma((2,)), dma((2,)),
        ],
        compiler_params=pltpu.CompilerParams(
            collective_id=0, has_side_effects=True, vmem_limit_bytes=60 * 2**20
        ),
    )(
        green_coeff,
        screened.reshape(total_k, 256),
        band_energy.T,
        time_basis,
        projector.T,
        memory_kernel,
        *tables,
    )


def solution(mesh):
    return jax.shard_map(
        on_device,
        mesh=mesh,
        in_specs=(P("ka", "ot", None), P(None, ("ot", "ka"), None), P("ka", None), P(), P(), P()),
        out_specs=(P("ka", "ot", None), P("ka", "ot", None)),
        check_vma=False,
    )
```

```python
import functools
import math

import jax
import jax.numpy as jnp
import numpy as np
from jax import lax
from jax.experimental import pallas as pl
from jax.experimental.pallas import tpu as pltpu
from jax.sharding import PartitionSpec as P

STEP_SIZE = 0.25
MESH = pl.DeviceIdType.MESH
BF = jnp.bfloat16
F32 = jnp.float32
PAD = 24


def phase_tables(lattice, block, group):
    kx_rows = group * block // lattice
    half = block // 2
    cosine = lambda a, b: np.cos(2.0 * math.pi * (a * b % lattice) / lattice)
    sine = lambda a, b: np.sin(2.0 * math.pi * (a * b % lattice) / lattice)
    idx = np.arange(lattice)
    cx, sx = cosine(idx[:, None], idx[None, :]), sine(idx[:, None], idx[None, :])
    x_fwd = np.kron(np.eye(3), np.concatenate([cx, sx], axis=0))
    x_inv = np.concatenate([cx, -sx], axis=1)
    row = np.arange(group * 2 * PAD)
    place, inner = row // PAD, row % PAD
    kk = (place // 2) * block + (place % 2) * half + inner
    valid = inner < half
    kx_of, ky_of = kk // lattice, kk % lattice
    lat_row = np.arange(kx_rows * lattice)
    rx_of, ry_of = lat_row // lattice, lat_row % lattice
    same = (rx_of[:, None] == kx_of[None, :]) & valid[None, :]
    cy = np.where(same, cosine(ry_of[:, None], ky_of[None, :]), 0.0)
    sy = np.where(same, sine(ry_of[:, None], ky_of[None, :]), 0.0)
    y_fwd = np.concatenate([cy, sy], axis=1)
    y_inv = np.concatenate([cy.T, -sy.T], axis=1)
    return [t.astype(np.float32) for t in (x_fwd, x_inv, y_fwd, y_inv)]


def split(value):
    high = value.astype(BF)
    return high, (value - high.astype(F32)).astype(BF)


def dot(left, right):
    return jnp.dot(left, right, preferred_element_type=F32)


def kernel(
    green_in, screen_in, energy_in, basis_in, proj_in, memk_in, xf_in, xi_in, yf_in, yi_in,
    sigma_ref, next_ref,
    green_ref, w_raw, energy_ref, basis_ref, proj_ref, memk_ref, xf_ref, xi_ref, yf_ref, yi_ref,
    fsem, plane_in, wre_full, wim_full, pages, packed1, landed1, packed2, landed2, ytab, utab, xbuf,
    tb, pb, pq, kb, pt, partner, gmat, amat, skm,
    lsem, ssem1, rsem1, ssem2, rsem2, psem, qsem,
):
    ka, ot = lax.axis_index("ka"), lax.axis_index("ot")
    half, orbital = ot % 2, ot // 2
    mine, place = ka // 4, half * 4 + ka % 4
    count_k, rows_m, width = green_ref.shape
    hk = count_k // 2

    def device_of(grp, slot):
        return (grp * 4 + slot % 4, orbital * 2 + slot // 4)

    def far(i):
        return 2 - i + 3 * (i // 2) - 2 * (i // 3)

    def to_group(i):
        return (mine // 4 + far(i // 4)) % 4 * 4 + (mine + far(i % 4)) % 4

    def from_group(i):
        return (mine // 4 + 4 - far(i // 4)) % 4 * 4 + (mine + 4 - far(i % 4)) % 4

    barrier = pltpu.get_barrier_semaphore()

    def tell(semaphore, grp, slot):
        pl.semaphore_signal(semaphore, inc=1, device_id=device_of(grp, slot), device_id_type=MESH)

    fetches = [
        pltpu.make_async_copy(source, target, fsem.at[i])
        for i, (source, target) in enumerate([
            (green_in, green_ref), (basis_in, basis_ref), (screen_in, w_raw),
            (energy_in, energy_ref), (proj_in, proj_ref), (memk_in, memk_ref),
            (xf_in, xf_ref), (xi_in, xi_ref), (yf_in, yf_ref), (yi_in, yi_ref),
        ])
    ]
    for fetch in fetches:
        fetch.start()
    for s in range(1, 16):
        tell(barrier, mine ^ s, place)
    for s in range(1, 8):
        tell(barrier, mine, place ^ s)
    pl.semaphore_wait(barrier, 22)
    for s in range(1, 8):
        tell(plane_in, mine, place ^ s)
    for fetch in fetches[:2]:
        fetch.wait()


    def swap(part):
        lo, hi = ((0, 18), (18, count_k))[part]
        return pltpu.make_async_remote_copy(
            src_ref=green_ref.at[pl.ds(lo, hi - lo)], dst_ref=partner.at[pl.ds(lo, hi - lo)],
            send_sem=psem.at[part], recv_sem=qsem.at[part],
            device_id=(ka, orbital * 2 + 1 - half), device_id_type=MESH,
        )

    swap(0).start()

    lane64 = lax.broadcasted_iota(jnp.int32, (1, width), 1)
    low64 = lane64 < 64
    low32 = lane64 % 64 < 32
    minus_low = jnp.where(low64, -1.0, 1.0).astype(F32)

    def times_i(value):
        return pltpu.roll(value, 64, 1) * minus_low

    basis_t = basis_ref[...].T
    t_high, t_low = split(basis_t)
    t_cat = jnp.concatenate([t_high, t_low], axis=1)

    def rows_step(r, carry):
        parts = []
        both = [green_ref[r].astype(F32), green_ref[hk + r].astype(F32)]
        turned = [pltpu.roll(v, 64, 1) for v in both]
        for v, u in zip(both, turned):
            parts.append(jnp.where(low64, v, u))
        for v, u in zip(both, turned):
            parts.append(jnp.where(low64, u, v))
        right = jnp.concatenate(parts, axis=0).astype(BF)
        out = lax.dot_general(
            t_cat, right, (((1,), (1,)), ((), ())), preferred_element_type=F32
        )
        pages[pl.ds(r, 128, stride=PAD), :] = out
        return carry

    for r in range(hk):
        rows_step(r, 0)

    pl.semaphore_wait(plane_in, 7)

    def pack1(t):
        grp = to_group(t)
        for slot in range(8):
            q = (slot // 4) * 64 + grp * 4 + slot % 4
            start = pl.multiple_of(q * PAD, 8)
            value = pages[pl.ds(start, hk), :].astype(BF)
            packed1[grp, slot] = value.reshape(hk // 2, 2, width)

    def send(packed, landed, sent, came, t, s):
        grp, slot = to_group(t), place ^ s
        pltpu.make_async_remote_copy(
            src_ref=packed.at[grp, slot], dst_ref=landed.at[mine, place],
            send_sem=sent, recv_sem=came.at[t],
            device_id=device_of(grp, slot), device_id_type=MESH,
        ).start()

    def send1(i, carry):
        for u in range(1):
            pack1(i * 1 + u)
        for s in (6, 2, 7, 3, 4, 5, 1, 0):
            for u in range(1):
                send(packed1, landed1, ssem1, rsem1, i * 1 + u, s)
        return carry

    lax.fori_loop(0, 15, send1, 0)
    pack1(15)
    for s in (6, 2, 7, 3, 4, 5, 1):
        send(packed1, landed1, ssem1, rsem1, 15, s)
    own1 = pltpu.make_async_copy(packed1.at[mine, place], landed1.at[mine, place], rsem1.at[15])
    own1.start()

    for fetch in fetches[2:]:
        fetch.wait()
    zeros = jnp.zeros((64, 128), F32)
    basis = basis_ref[...]
    wide = jnp.concatenate(
        [jnp.concatenate([basis, zeros], axis=1), jnp.concatenate([zeros, basis], axis=1)], axis=0
    )
    high, low = split(wide)
    tb[0:128, :] = high
    tb[128:256, :] = low
    proj = proj_ref[...].T
    blank = jnp.zeros((128, 64), F32)
    left, right = jnp.concatenate([proj, blank], axis=1), jnp.concatenate([blank, proj], axis=1)
    for offset, piece in ((0, left), (128, right)):
        high, low = split(piece)
        pb[offset:offset + 128, :] = high
        pb[256 + offset:256 + offset + 128, :] = low
    pt[0:128, :] = left
    for grp in range(16):
        for h in range(2):
            pt[pl.ds(128 + grp * 8 + h * 4, 4), :] = pt[pl.ds(h * 64 + grp * 4, 4), :]
    left = pt[128:256, :]
    right = pltpu.roll(left, 64, 1)
    for offset, piece in ((0, left), (128, right)):
        high, low = split(piece)
        pq[offset:offset + 128, :] = high
        pq[256 + offset:256 + offset + 128, :] = low
    memk = memk_ref[...]
    blank = jnp.zeros((64, 64), F32)
    wide = jnp.concatenate(
        [jnp.concatenate([memk, blank], axis=1), jnp.concatenate([blank, memk], axis=1)], axis=0
    )
    high, low = split(wide)
    kb[0:128, :] = high
    kb[128:256, :] = low
    scale = 1.0 / w_raw.shape[0]

    def widen(i, carry):
        value = w_raw[pl.ds(pl.multiple_of(i * 48, 16), 48), :].astype(F32) * scale
        wre_full[pl.ds(i, 48, stride=48), :] = value[:, :128]
        wim_full[pl.ds(i, 48, stride=48), :] = value[:, 128:]
        return carry

    lax.fori_loop(0, 48, widen, 0)
    xbuf[...] = jnp.zeros_like(xbuf)

    def arrive1(t, carry):
        grp = from_group(t)

        ref = landed1.at[grp]
        pltpu.make_async_copy(ref, ref, rsem1.at[t]).wait()

        for i in range(4):
            v0 = landed1[grp, i].reshape(hk, width).astype(F32)
            v1 = landed1[grp, 4 + i].reshape(hk, width).astype(F32)
            xbuf[i * 2 * PAD:i * 2 * PAD + hk, :] = jnp.where(low32, v0, pltpu.roll(v1, 32, 1))
            xbuf[i * 2 * PAD + PAD:i * 2 * PAD + PAD + hk, :] = jnp.where(
                low32, pltpu.roll(v0, 96, 1), v1
            )
        value = xbuf[...]
        stacked = jnp.concatenate([value.astype(BF), times_i(value).astype(BF)], axis=0)
        out = dot(yf_ref[...], stacked)
        for u in range(3):
            ytab[pl.ds(grp * 3 + u, 48, stride=48), :] = out[u * 48:u * 48 + 48]
        return carry

    lax.fori_loop(0, 16, arrive1, 0)

    swap(1).start()

    together = 24

    def along_x(values, sign):
        done = []
        for u in range(0, len(values), 2 * 3):
            sides = [
                jnp.concatenate([v.astype(BF) for v in values[at:at + 3]], axis=0)
                for at in (u, u + 3)
            ]
            out = dot(xf_ref[...], jnp.concatenate(sides, axis=1))
            for v in range(2):
                for at in range(0, 96 * 3, 96):
                    even = out[at:at + 48, v * 128:v * 128 + 128]
                    odd = out[at + 48:at + 96, v * 128:v * 128 + 128]
                    done.append(even + pltpu.roll(odd, 64, 1) * (minus_low * sign))
        return done


    def distances(step, carry):
        near_in = along_x(
            [ytab[pl.ds(pl.multiple_of((step * together + u) * 48, 8), 48), :] for u in range(together)],
            1.0,
        )
        near_in = [v.astype(BF) for v in near_in]
        near_in = jnp.concatenate(near_in, axis=0)
        near = dot(jnp.concatenate([near_in, near_in], axis=1), tb[...])
        far_parts = []
        for u in range(together):
            ry = step * together + u
            w_re = wre_full[pl.ds(pl.multiple_of(ry * 48, 8), 48), :]
            w_im = wim_full[pl.ds(pl.multiple_of(ry * 48, 8), 48), :]
            n_re, n_im = near[u * 48:u * 48 + 48, :128], near[u * 48:u * 48 + 48, 128:]
            far_re = -(n_re * w_im + n_im * w_re)
            far_im = n_re * w_re - n_im * w_im
            far_parts.append(jnp.concatenate([far_re.astype(BF), far_im.astype(BF)], axis=1))
        far = jnp.concatenate(far_parts, axis=0)
        home = dot(far, pb[0:256, :]) + dot(far, pb[256:512, :])
        back = along_x([home[u * 48:u * 48 + 48, :] for u in range(together)], -1.0)
        for u in range(together):
            utab[pl.ds(pl.multiple_of((step * together + u) * 48, 8), 48), :] = back[u]
        return carry

    lax.fori_loop(0, 48 // together, distances, 0)

    def pack2(t):
        grp = to_group(t)
        value = jnp.concatenate(
            [utab[pl.ds(grp * 3 + u, 48, stride=48), :] for u in range(3)], axis=0
        )
        stacked = jnp.concatenate([value.astype(BF), times_i(value).astype(BF)], axis=0)
        out = dot(yi_ref[...], stacked)
        for i in range(4):
            v0 = out[i * 2 * PAD:i * 2 * PAD + PAD]
            v1 = out[i * 2 * PAD + PAD:i * 2 * PAD + 2 * PAD]
            first = jnp.where(low32, v0, pltpu.roll(v1, 32, 1))
            second = jnp.where(low32, pltpu.roll(v0, 96, 1), v1)
            packed2[grp, i] = first[:hk].astype(BF).reshape(hk // 2, 2, width)
            packed2[grp, 4 + i] = second[:hk].astype(BF).reshape(hk // 2, 2, width)

    def send2(i, carry):
        for u in range(1):
            pack2(i * 1 + u)
        for s in (6, 2, 7, 3, 4, 5, 1, 0):
            for u in range(1):
                send(packed2, landed2, ssem2, rsem2, i * 1 + u, s)
        return carry

    lax.fori_loop(0, 15, send2, 0)
    pack2(15)
    for s in (6, 2, 7, 3, 4, 5, 1):
        send(packed2, landed2, ssem2, rsem2, 15, s)
    own2 = pltpu.make_async_copy(packed2.at[mine, place], landed2.at[mine, place], rsem2.at[15])
    own2.start()

    swap(0).wait()
    swap(1).wait()
    mine_at = pl.multiple_of(half * rows_m, 32)
    other_at = pl.multiple_of((1 - half) * rows_m, 32)

    def build(k, carry):
        for ref, at in ((green_ref, mine_at), (partner, other_at)):
            value = ref[k]
            turned = (pltpu.roll(value.astype(F32), 64, 1) * -minus_low).astype(BF)
            gmat[k, pl.ds(at, rows_m), :] = turned
            gmat[k, pl.ds(64 + at, rows_m), :] = value
        return carry

    lax.fori_loop(0, count_k, build, 0)

    def arrive2(t, carry):
        grp = from_group(t)

        ref = landed2.at[grp]
        pltpu.make_async_copy(ref, ref, rsem2.at[t]).wait()

        for slot in range(8):
            value = landed2[grp, slot].reshape(hk, width).astype(F32)
            start = pl.multiple_of((grp * 8 + slot) * PAD, 8)
            pages[pl.ds(start, hk), :] = value
        return carry

    lax.fori_loop(0, 16, arrive2, 0)

    for r in range(hk):
        value = pages[pl.ds(r, 128, stride=PAD), :].T.astype(BF)
        for k2 in range(2):
            amat[(k2 * hk + r) * rows_m:(k2 * hk + r + 1) * rows_m, 0:128] = value[
                k2 * 32:k2 * 32 + 32
            ]
            amat[(k2 * hk + r) * rows_m:(k2 * hk + r + 1) * rows_m, 128:256] = value[
                64 + k2 * 32:64 + k2 * 32 + 32
            ]

    def coeffs(i, carry):
        at = pl.multiple_of(i * 1152, 32)
        value = amat[pl.ds(at, 1152), :]
        sigma = (dot(value, pq[0:256, :]) + dot(value, pq[256:512, :])).astype(BF)
        sigma_ref[pl.ds(i * 36, 36)] = sigma.reshape(36, rows_m, width)
        skm[pl.ds(at, 1152), :] = dot(jnp.concatenate([sigma, sigma], axis=1), kb[...]).astype(BF)
        for u in range(36):
            k = i * 36 + u
            row = pl.multiple_of(i * 1152 + u * 32, 32)
            memory = dot(skm[pl.ds(row, rows_m), :], gmat[k])
            turned = gmat[k, pl.ds(mine_at, rows_m), :].astype(F32)
            own = green_ref[k].astype(F32)
            energy = energy_ref[orbital, k]
            next_ref[k] = (own + STEP_SIZE * (energy * turned + memory)).astype(BF)
        return carry

    lax.fori_loop(0, count_k // 36, coeffs, 0)

    ref = landed1.at[pl.ds(0, 15)]
    pltpu.make_async_copy(ref, ref, ssem1).wait()
    ref = landed1.at[0, pl.ds(0, 7)]
    pltpu.make_async_copy(ref, ref, ssem1).wait()
    ref = landed2.at[pl.ds(0, 15)]
    pltpu.make_async_copy(ref, ref, ssem2).wait()
    ref = landed2.at[0, pl.ds(0, 7)]
    pltpu.make_async_copy(ref, ref, ssem2).wait()


def on_device(green_coeff, screened, band_energy, time_basis, projector, memory_kernel):
    total_k = screened.shape[0]
    tables = [jnp.asarray(t, BF) for t in phase_tables(48, green_coeff.shape[0], 4)]
    vmem = pl.BlockSpec(memory_space=pltpu.VMEM)
    dma = pltpu.SemaphoreType.DMA
    message = (16, 8, 9, 2, 128)
    out = pltpu.VMEM(green_coeff.shape, BF)
    return pl.pallas_call(
        kernel,
        out_shape=(out, out),
        in_specs=[pl.BlockSpec(memory_space=pl.ANY)] * 10,
        out_specs=(vmem, vmem),
        scratch_shapes=[
            pltpu.VMEM(green_coeff.shape, BF),
            pltpu.VMEM((total_k, 256), BF),
            pltpu.SMEM((2, green_coeff.shape[0]), F32),
            pltpu.VMEM(time_basis.shape, F32),
            pltpu.VMEM(time_basis.shape, F32),
            pltpu.VMEM(memory_kernel.shape, F32),
            *[pltpu.VMEM(t.shape, BF) for t in tables],
            dma((10,)),
            pltpu.SemaphoreType.REGULAR,
            pltpu.VMEM((total_k, 128), F32),
            pltpu.VMEM((total_k, 128), F32),
            pltpu.VMEM((128 * PAD, 128), F32),
            pltpu.VMEM(message, BF),
            pltpu.VMEM(message, BF),
            pltpu.VMEM(message, BF),
            pltpu.VMEM(message, BF),
            pltpu.VMEM((total_k, 128), F32),
            pltpu.VMEM((total_k, 128), F32),
            pltpu.VMEM((8 * PAD, 128), F32),
            pltpu.VMEM((256, 256), BF),
            pltpu.VMEM((512, 128), BF),
            pltpu.VMEM((512, 128), BF),
            pltpu.VMEM((256, 128), BF),
            pltpu.VMEM((256, 128), F32),
            pltpu.VMEM(green_coeff.shape, BF),
            pltpu.VMEM((36, 128, 128), BF),
            pltpu.VMEM((1152, 256), BF),
            pltpu.VMEM((1152, 128), BF),
            dma, dma, dma((16,)), dma, dma((16,)), dma((2,)), dma((2,)),
        ],
        compiler_params=pltpu.CompilerParams(
            collective_id=0, has_side_effects=True, vmem_limit_bytes=60 * 2**20
        ),
    )(
        green_coeff,
        screened.reshape(total_k, 256),
        band_energy.T,
        time_basis,
        projector.T,
        memory_kernel,
        *tables,
    )


def solution(mesh):
    return jax.shard_map(
        on_device,
        mesh=mesh,
        in_specs=(P("ka", "ot", None), P(None, ("ot", "ka"), None), P("ka", None), P(), P(), P()),
        out_specs=(P("ka", "ot", None), P("ka", "ot", None)),
        check_vma=False,
    )
```

```python
import functools
import math

import jax
import jax.numpy as jnp
import numpy as np
from jax import lax
from jax.experimental import pallas as pl
from jax.experimental.pallas import tpu as pltpu
from jax.sharding import PartitionSpec as P

STEP_SIZE = 0.25
MESH = pl.DeviceIdType.MESH
BF = jnp.bfloat16
F32 = jnp.float32
PAD = 24


def phase_tables(lattice, block, group):
    kx_rows = group * block // lattice
    half = block // 2
    cosine = lambda a, b: np.cos(2.0 * math.pi * (a * b % lattice) / lattice)
    sine = lambda a, b: np.sin(2.0 * math.pi * (a * b % lattice) / lattice)
    idx = np.arange(lattice)
    cx, sx = cosine(idx[:, None], idx[None, :]), sine(idx[:, None], idx[None, :])
    x_fwd = np.kron(np.eye(3), np.concatenate([cx, sx], axis=0))
    x_inv = np.concatenate([cx, -sx], axis=1)
    row = np.arange(group * 2 * PAD)
    place, inner = row // PAD, row % PAD
    kk = (place // 2) * block + (place % 2) * half + inner
    valid = inner < half
    kx_of, ky_of = kk // lattice, kk % lattice
    lat_row = np.arange(kx_rows * lattice)
    rx_of, ry_of = lat_row // lattice, lat_row % lattice
    same = (rx_of[:, None] == kx_of[None, :]) & valid[None, :]
    cy = np.where(same, cosine(ry_of[:, None], ky_of[None, :]), 0.0)
    sy = np.where(same, sine(ry_of[:, None], ky_of[None, :]), 0.0)
    y_fwd = np.concatenate([cy, sy], axis=1)
    y_inv = np.concatenate([cy.T, -sy.T], axis=1)
    return [t.astype(np.float32) for t in (x_fwd, x_inv, y_fwd, y_inv)]


def split(value):
    high = value.astype(BF)
    return high, (value - high.astype(F32)).astype(BF)


def dot(left, right):
    return jnp.dot(left, right, preferred_element_type=F32)


def kernel(
    green_in, screen_in, energy_in, basis_in, proj_in, memk_in, xf_in, xi_in, yf_in, yi_in,
    both_ref,
    green_ref, w_raw, energy_ref, basis_ref, proj_ref, memk_ref, xf_ref, xi_ref, yf_ref, yi_ref,
    fsem, plane_in, wre_full, wim_full, pages, packed1, landed1, packed2, landed2, ytab, utab, xbuf,
    tb, pb, pq, kb, pt, partner, gmat, amat, skm,
    lsem, ssem1, rsem1, ssem2, rsem2, psem, qsem,
):
    ka, ot = lax.axis_index("ka"), lax.axis_index("ot")
    half, orbital = ot % 2, ot // 2
    mine, place = ka // 4, half * 4 + ka % 4
    count_k, rows_m, width = green_ref.shape
    hk = count_k // 2

    def device_of(grp, slot):
        return (grp * 4 + slot % 4, orbital * 2 + slot // 4)

    def far(i):
        return 2 - i + 3 * (i // 2) - 2 * (i // 3)

    def to_group(i):
        return (mine // 4 + far(i // 4)) % 4 * 4 + (mine + far(i % 4)) % 4

    def from_group(i):
        return (mine // 4 + 4 - far(i // 4)) % 4 * 4 + (mine + 4 - far(i % 4)) % 4

    barrier = pltpu.get_barrier_semaphore()

    def tell(semaphore, grp, slot):
        pl.semaphore_signal(semaphore, inc=1, device_id=device_of(grp, slot), device_id_type=MESH)

    fetches = [
        pltpu.make_async_copy(source, target, fsem.at[i])
        for i, (source, target) in enumerate([
            (green_in, green_ref), (basis_in, basis_ref), (screen_in, w_raw),
            (energy_in, energy_ref), (proj_in, proj_ref), (memk_in, memk_ref),
            (xf_in, xf_ref), (xi_in, xi_ref), (yf_in, yf_ref), (yi_in, yi_ref),
        ])
    ]
    for fetch in fetches:
        fetch.start()
    for s in range(1, 16):
        tell(barrier, mine ^ s, place)
    for s in range(1, 8):
        tell(barrier, mine, place ^ s)
    pl.semaphore_wait(barrier, 22)
    for s in range(1, 8):
        tell(plane_in, mine, place ^ s)
    for fetch in fetches[:2]:
        fetch.wait()


    def swap(part):
        lo, hi = ((0, 18), (18, count_k))[part]
        return pltpu.make_async_remote_copy(
            src_ref=green_ref.at[pl.ds(lo, hi - lo)], dst_ref=partner.at[pl.ds(lo, hi - lo)],
            send_sem=psem.at[part], recv_sem=qsem.at[part],
            device_id=(ka, orbital * 2 + 1 - half), device_id_type=MESH,
        )

    swap(0).start()

    lane64 = lax.broadcasted_iota(jnp.int32, (1, width), 1)
    low64 = lane64 < 64
    low32 = lane64 % 64 < 32
    minus_low = jnp.where(low64, -1.0, 1.0).astype(F32)

    def times_i(value):
        return pltpu.roll(value, 64, 1) * minus_low

    basis_t = basis_ref[...].T
    t_high, t_low = split(basis_t)
    t_cat = jnp.concatenate([t_high, t_low], axis=1)

    def rows_step(r, carry):
        parts = []
        both = [green_ref[r].astype(F32), green_ref[hk + r].astype(F32)]
        turned = [pltpu.roll(v, 64, 1) for v in both]
        for v, u in zip(both, turned):
            parts.append(jnp.where(low64, v, u))
        for v, u in zip(both, turned):
            parts.append(jnp.where(low64, u, v))
        right = jnp.concatenate(parts, axis=0).astype(BF)
        out = lax.dot_general(
            t_cat, right, (((1,), (1,)), ((), ())), preferred_element_type=F32
        )
        pages[pl.ds(r, 128, stride=PAD), :] = out
        return carry

    for r in range(hk):
        rows_step(r, 0)

    pl.semaphore_wait(plane_in, 7)

    def pack1(t):
        grp = to_group(t)
        for slot in range(8):
            q = (slot // 4) * 64 + grp * 4 + slot % 4
            start = pl.multiple_of(q * PAD, 8)
            value = pages[pl.ds(start, hk), :].astype(BF)
            packed1[grp, slot] = value.reshape(hk // 2, 2, width)

    def send(packed, landed, sent, came, t, s):
        grp, slot = to_group(t), place ^ s
        pltpu.make_async_remote_copy(
            src_ref=packed.at[grp, slot], dst_ref=landed.at[mine, place],
            send_sem=sent, recv_sem=came.at[t],
            device_id=device_of(grp, slot), device_id_type=MESH,
        ).start()

    def send1(i, carry):
        for u in range(1):
            pack1(i * 1 + u)
        for s in (6, 2, 7, 3, 4, 5, 1, 0):
            for u in range(1):
                send(packed1, landed1, ssem1, rsem1, i * 1 + u, s)
        return carry

    lax.fori_loop(0, 15, send1, 0)
    pack1(15)
    for s in (6, 2, 7, 3, 4, 5, 1):
        send(packed1, landed1, ssem1, rsem1, 15, s)
    own1 = pltpu.make_async_copy(packed1.at[mine, place], landed1.at[mine, place], rsem1.at[15])
    own1.start()

    for fetch in fetches[2:]:
        fetch.wait()
    zeros = jnp.zeros((64, 128), F32)
    basis = basis_ref[...]
    wide = jnp.concatenate(
        [jnp.concatenate([basis, zeros], axis=1), jnp.concatenate([zeros, basis], axis=1)], axis=0
    )
    high, low = split(wide)
    tb[0:128, :] = high
    tb[128:256, :] = low
    proj = proj_ref[...].T
    blank = jnp.zeros((128, 64), F32)
    left, right = jnp.concatenate([proj, blank], axis=1), jnp.concatenate([blank, proj], axis=1)
    for offset, piece in ((0, left), (128, right)):
        high, low = split(piece)
        pb[offset:offset + 128, :] = high
        pb[256 + offset:256 + offset + 128, :] = low
    pt[0:128, :] = left
    for grp in range(16):
        for h in range(2):
            pt[pl.ds(128 + grp * 8 + h * 4, 4), :] = pt[pl.ds(h * 64 + grp * 4, 4), :]
    left = pt[128:256, :]
    right = pltpu.roll(left, 64, 1)
    for offset, piece in ((0, left), (128, right)):
        high, low = split(piece)
        pq[offset:offset + 128, :] = high
        pq[256 + offset:256 + offset + 128, :] = low
    memk = memk_ref[...]
    blank = jnp.zeros((64, 64), F32)
    wide = jnp.concatenate(
        [jnp.concatenate([memk, blank], axis=1), jnp.concatenate([blank, memk], axis=1)], axis=0
    )
    high, low = split(wide)
    kb[0:128, :] = high
    kb[128:256, :] = low
    scale = 1.0 / w_raw.shape[0]

    def widen(i, carry):
        value = w_raw[pl.ds(pl.multiple_of(i * 48, 16), 48), :].astype(F32) * scale
        wre_full[pl.ds(i, 48, stride=48), :] = value[:, :128]
        wim_full[pl.ds(i, 48, stride=48), :] = value[:, 128:]
        return carry

    lax.fori_loop(0, 48, widen, 0)
    xbuf[...] = jnp.zeros_like(xbuf)

    def arrive1(t, carry):
        grp = from_group(t)

        ref = landed1.at[grp]
        pltpu.make_async_copy(ref, ref, rsem1.at[t]).wait()

        for i in range(4):
            v0 = landed1[grp, i].reshape(hk, width).astype(F32)
            v1 = landed1[grp, 4 + i].reshape(hk, width).astype(F32)
            xbuf[i * 2 * PAD:i * 2 * PAD + hk, :] = jnp.where(low32, v0, pltpu.roll(v1, 32, 1))
            xbuf[i * 2 * PAD + PAD:i * 2 * PAD + PAD + hk, :] = jnp.where(
                low32, pltpu.roll(v0, 96, 1), v1
            )
        value = xbuf[...]
        stacked = jnp.concatenate([value.astype(BF), times_i(value).astype(BF)], axis=0)
        out = dot(yf_ref[...], stacked)
        for u in range(3):
            ytab[pl.ds(grp * 3 + u, 48, stride=48), :] = out[u * 48:u * 48 + 48]
        return carry

    lax.fori_loop(0, 16, arrive1, 0)

    swap(1).start()

    together = 24

    def along_x(values, sign):
        done = []
        for u in range(0, len(values), 2 * 3):
            sides = [
                jnp.concatenate([v.astype(BF) for v in values[at:at + 3]], axis=0)
                for at in (u, u + 3)
            ]
            out = dot(xf_ref[...], jnp.concatenate(sides, axis=1))
            for v in range(2):
                for at in range(0, 96 * 3, 96):
                    even = out[at:at + 48, v * 128:v * 128 + 128]
                    odd = out[at + 48:at + 96, v * 128:v * 128 + 128]
                    done.append(even + pltpu.roll(odd, 64, 1) * (minus_low * sign))
        return done


    def distances(step, carry):
        near_in = along_x(
            [ytab[pl.ds(pl.multiple_of((step * together + u) * 48, 8), 48), :] for u in range(together)],
            1.0,
        )
        near_in = [v.astype(BF) for v in near_in]
        near_in = jnp.concatenate(near_in, axis=0)
        near = dot(jnp.concatenate([near_in, near_in], axis=1), tb[...])
        far_parts = []
        for u in range(together):
            ry = step * together + u
            w_re = wre_full[pl.ds(pl.multiple_of(ry * 48, 8), 48), :]
            w_im = wim_full[pl.ds(pl.multiple_of(ry * 48, 8), 48), :]
            n_re, n_im = near[u * 48:u * 48 + 48, :128], near[u * 48:u * 48 + 48, 128:]
            far_re = -(n_re * w_im + n_im * w_re)
            far_im = n_re * w_re - n_im * w_im
            far_parts.append(jnp.concatenate([far_re.astype(BF), far_im.astype(BF)], axis=1))
        far = jnp.concatenate(far_parts, axis=0)
        home = dot(far, pb[0:256, :]) + dot(far, pb[256:512, :])
        back = along_x([home[u * 48:u * 48 + 48, :] for u in range(together)], -1.0)
        for u in range(together):
            utab[pl.ds(pl.multiple_of((step * together + u) * 48, 8), 48), :] = back[u]
        return carry

    lax.fori_loop(0, 48 // together, distances, 0)

    def pack2(t):
        grp = to_group(t)
        value = jnp.concatenate(
            [utab[pl.ds(grp * 3 + u, 48, stride=48), :] for u in range(3)], axis=0
        )
        stacked = jnp.concatenate([value.astype(BF), times_i(value).astype(BF)], axis=0)
        out = dot(yi_ref[...], stacked)
        for i in range(4):
            v0 = out[i * 2 * PAD:i * 2 * PAD + PAD]
            v1 = out[i * 2 * PAD + PAD:i * 2 * PAD + 2 * PAD]
            first = jnp.where(low32, v0, pltpu.roll(v1, 32, 1))
            second = jnp.where(low32, pltpu.roll(v0, 96, 1), v1)
            packed2[grp, i] = first[:hk].astype(BF).reshape(hk // 2, 2, width)
            packed2[grp, 4 + i] = second[:hk].astype(BF).reshape(hk // 2, 2, width)

    def send2(i, carry):
        for u in range(1):
            pack2(i * 1 + u)
        for s in (6, 2, 7, 3, 4, 5, 1, 0):
            for u in range(1):
                send(packed2, landed2, ssem2, rsem2, i * 1 + u, s)
        return carry

    lax.fori_loop(0, 15, send2, 0)
    pack2(15)
    for s in (6, 2, 7, 3, 4, 5, 1):
        send(packed2, landed2, ssem2, rsem2, 15, s)
    own2 = pltpu.make_async_copy(packed2.at[mine, place], landed2.at[mine, place], rsem2.at[15])
    own2.start()

    swap(0).wait()
    swap(1).wait()
    mine_at = pl.multiple_of(half * rows_m, 32)
    other_at = pl.multiple_of((1 - half) * rows_m, 32)

    def build(k, carry):
        for ref, at in ((green_ref, mine_at), (partner, other_at)):
            value = ref[k]
            turned = (pltpu.roll(value.astype(F32), 64, 1) * -minus_low).astype(BF)
            gmat[k, pl.ds(at, rows_m), :] = turned
            gmat[k, pl.ds(64 + at, rows_m), :] = value
        return carry

    lax.fori_loop(0, count_k, build, 0)

    def arrive2(t, carry):
        grp = from_group(t)

        ref = landed2.at[grp]
        pltpu.make_async_copy(ref, ref, rsem2.at[t]).wait()

        for slot in range(8):
            value = landed2[grp, slot].reshape(hk, width).astype(F32)
            start = pl.multiple_of((grp * 8 + slot) * PAD, 8)
            pages[pl.ds(start, hk), :] = value
        return carry

    lax.fori_loop(0, 16, arrive2, 0)

    for r in range(hk):
        value = pages[pl.ds(r, 128, stride=PAD), :].T.astype(BF)
        for k2 in range(2):
            amat[(k2 * hk + r) * rows_m:(k2 * hk + r + 1) * rows_m, 0:128] = value[
                k2 * 32:k2 * 32 + 32
            ]
            amat[(k2 * hk + r) * rows_m:(k2 * hk + r + 1) * rows_m, 128:256] = value[
                64 + k2 * 32:64 + k2 * 32 + 32
            ]

    def coeffs(i, carry):
        at = pl.multiple_of(i * 1152, 32)
        value = amat[pl.ds(at, 1152), :]
        sigma = (dot(value, pq[0:256, :]) + dot(value, pq[256:512, :])).astype(BF)
        both_ref[:, :, 0:128] = sigma.reshape(36, rows_m, width).astype(F32)
        skm[pl.ds(at, 1152), :] = dot(jnp.concatenate([sigma, sigma], axis=1), kb[...]).astype(BF)
        for u in range(0, 36, 2):
            pair = dot(
                skm[u * 32:u * 32 + 64, :], jnp.concatenate([gmat[u], gmat[u + 1]], axis=1)
            )
            for k, memory in ((u, pair[:rows_m, :128]), (u + 1, pair[rows_m:, 128:])):
                turned = gmat[k, pl.ds(mine_at, rows_m), :].astype(F32)
                own = green_ref[k].astype(F32)
                energy = energy_ref[orbital, k]
                both_ref[k, :, 128:256] = own + STEP_SIZE * (energy * turned + memory)
        return carry

    lax.fori_loop(0, count_k // 36, coeffs, 0)

    ref = landed1.at[pl.ds(0, 15)]
    pltpu.make_async_copy(ref, ref, ssem1).wait()
    ref = landed1.at[0, pl.ds(0, 7)]
    pltpu.make_async_copy(ref, ref, ssem1).wait()
    ref = landed2.at[pl.ds(0, 15)]
    pltpu.make_async_copy(ref, ref, ssem2).wait()
    ref = landed2.at[0, pl.ds(0, 7)]
    pltpu.make_async_copy(ref, ref, ssem2).wait()


def on_device(green_coeff, screened, band_energy, time_basis, projector, memory_kernel):
    total_k = screened.shape[0]
    tables = [jnp.asarray(t, BF) for t in phase_tables(48, green_coeff.shape[0], 4)]
    vmem = pl.BlockSpec(memory_space=pltpu.VMEM)
    dma = pltpu.SemaphoreType.DMA
    message = (16, 8, 9, 2, 128)
    out = pltpu.VMEM((36, 32, 256), F32)
    both = pl.pallas_call(
        kernel,
        out_shape=out,
        in_specs=[pl.BlockSpec(memory_space=pl.ANY)] * 10,
        out_specs=vmem,
        scratch_shapes=[
            pltpu.VMEM(green_coeff.shape, BF),
            pltpu.VMEM((total_k, 256), BF),
            pltpu.SMEM((2, green_coeff.shape[0]), F32),
            pltpu.VMEM(time_basis.shape, F32),
            pltpu.VMEM(time_basis.shape, F32),
            pltpu.VMEM(memory_kernel.shape, F32),
            *[pltpu.VMEM(t.shape, BF) for t in tables],
            dma((10,)),
            pltpu.SemaphoreType.REGULAR,
            pltpu.VMEM((total_k, 128), F32),
            pltpu.VMEM((total_k, 128), F32),
            pltpu.VMEM((128 * PAD, 128), F32),
            pltpu.VMEM(message, BF),
            pltpu.VMEM(message, BF),
            pltpu.VMEM(message, BF),
            pltpu.VMEM(message, BF),
            pltpu.VMEM((total_k, 128), F32),
            pltpu.VMEM((total_k, 128), F32),
            pltpu.VMEM((8 * PAD, 128), F32),
            pltpu.VMEM((256, 256), BF),
            pltpu.VMEM((512, 128), BF),
            pltpu.VMEM((512, 128), BF),
            pltpu.VMEM((256, 128), BF),
            pltpu.VMEM((256, 128), F32),
            pltpu.VMEM(green_coeff.shape, BF),
            pltpu.VMEM((36, 128, 128), BF),
            pltpu.VMEM((1152, 256), BF),
            pltpu.VMEM((1152, 128), BF),
            dma, dma, dma((16,)), dma, dma((16,)), dma((2,)), dma((2,)),
        ],
        compiler_params=pltpu.CompilerParams(
            collective_id=0, has_side_effects=True, vmem_limit_bytes=60 * 2**20
        ),
    )(
        green_coeff,
        screened.reshape(total_k, 256),
        band_energy.T,
        time_basis,
        projector.T,
        memory_kernel,
        *tables,
    )
    return both[:, :, :128].astype(BF), both[:, :, 128:].astype(BF)


def solution(mesh):
    return jax.shard_map(
        on_device,
        mesh=mesh,
        in_specs=(P("ka", "ot", None), P(None, ("ot", "ka"), None), P("ka", None), P(), P(), P()),
        out_specs=(P("ka", "ot", None), P("ka", "ot", None)),
        check_vma=False,
    )
```

```python
import functools
import math

import jax
import jax.numpy as jnp
import numpy as np
from jax import lax
from jax.experimental import pallas as pl
from jax.experimental.pallas import tpu as pltpu
from jax.sharding import PartitionSpec as P

STEP_SIZE = 0.25
MESH = pl.DeviceIdType.MESH
BF = jnp.bfloat16
F32 = jnp.float32
PAD = 24


def phase_tables(lattice, block, group):
    kx_rows = group * block // lattice
    half = block // 2
    cosine = lambda a, b: np.cos(2.0 * math.pi * (a * b % lattice) / lattice)
    sine = lambda a, b: np.sin(2.0 * math.pi * (a * b % lattice) / lattice)
    idx = np.arange(lattice)
    cx, sx = cosine(idx[:, None], idx[None, :]), sine(idx[:, None], idx[None, :])
    x_fwd = np.kron(np.eye(3), np.concatenate([cx, sx], axis=0))
    x_inv = np.concatenate([cx, -sx], axis=1)
    row = np.arange(group * 2 * PAD)
    place, inner = row // PAD, row % PAD
    kk = (place // 2) * block + (place % 2) * half + inner
    valid = inner < half
    kx_of, ky_of = kk // lattice, kk % lattice
    lat_row = np.arange(kx_rows * lattice)
    rx_of, ry_of = lat_row // lattice, lat_row % lattice
    same = (rx_of[:, None] == kx_of[None, :]) & valid[None, :]
    cy = np.where(same, cosine(ry_of[:, None], ky_of[None, :]), 0.0)
    sy = np.where(same, sine(ry_of[:, None], ky_of[None, :]), 0.0)
    y_fwd = np.concatenate([cy, sy], axis=1)
    y_inv = np.concatenate([cy.T, -sy.T], axis=1)
    return [t.astype(np.float32) for t in (x_fwd, x_inv, y_fwd, y_inv)]


def split(value):
    high = value.astype(BF)
    return high, (value - high.astype(F32)).astype(BF)


def dot(left, right):
    return jnp.dot(left, right, preferred_element_type=F32)


def kernel(
    green_in, screen_in, energy_in, basis_in, proj_in, memk_in, xf_in, xi_in, yf_in, yi_in,
    both_ref,
    green_ref, w_raw, energy_ref, basis_ref, proj_ref, memk_ref, xf_ref, xi_ref, yf_ref, yi_ref,
    fsem, plane_in, wre_full, wim_full, pages, packed1, landed1, packed2, landed2, ytab, utab, xbuf,
    tb, pb, pq, kb, pt, partner, gmat, amat, skm,
    lsem, ssem1, rsem1, ssem2, rsem2, psem, qsem,
):
    ka, ot = lax.axis_index("ka"), lax.axis_index("ot")
    half, orbital = ot % 2, ot // 2
    mine, place = ka // 4, half * 4 + ka % 4
    count_k, rows_m, width = green_ref.shape
    hk = count_k // 2

    def device_of(grp, slot):
        return (grp * 4 + slot % 4, orbital * 2 + slot // 4)

    def far(i):
        return 2 - i + 3 * (i // 2) - 2 * (i // 3)

    def to_group(i):
        return (mine // 4 + far(i // 4)) % 4 * 4 + (mine + far(i % 4)) % 4

    def from_group(i):
        return (mine // 4 + 4 - far(i // 4)) % 4 * 4 + (mine + 4 - far(i % 4)) % 4

    barrier = pltpu.get_barrier_semaphore()

    def tell(semaphore, grp, slot):
        pl.semaphore_signal(semaphore, inc=1, device_id=device_of(grp, slot), device_id_type=MESH)

    fetches = [
        pltpu.make_async_copy(source, target, fsem.at[i])
        for i, (source, target) in enumerate([
            (green_in, green_ref), (basis_in, basis_ref), (screen_in, w_raw),
            (energy_in, energy_ref), (proj_in, proj_ref), (memk_in, memk_ref),
            (xf_in, xf_ref), (xi_in, xi_ref), (yf_in, yf_ref), (yi_in, yi_ref),
        ])
    ]
    for fetch in fetches:
        fetch.start()
    for s in range(1, 16):
        tell(barrier, mine ^ s, place)
    for s in range(1, 8):
        tell(barrier, mine, place ^ s)
    pl.semaphore_wait(barrier, 22)
    for s in range(1, 8):
        tell(plane_in, mine, place ^ s)
    for fetch in fetches[:2]:
        fetch.wait()


    def swap(part):
        lo, hi = ((0, 18), (18, count_k))[part]
        return pltpu.make_async_remote_copy(
            src_ref=green_ref.at[pl.ds(lo, hi - lo)], dst_ref=partner.at[pl.ds(lo, hi - lo)],
            send_sem=psem.at[part], recv_sem=qsem.at[part],
            device_id=(ka, orbital * 2 + 1 - half), device_id_type=MESH,
        )

    swap(0).start()

    lane64 = lax.broadcasted_iota(jnp.int32, (1, width), 1)
    low64 = lane64 < 64
    low32 = lane64 % 64 < 32
    minus_low = jnp.where(low64, -1.0, 1.0).astype(F32)

    def times_i(value):
        return pltpu.roll(value, 64, 1) * minus_low

    basis_t = basis_ref[...].T
    t_high, t_low = split(basis_t)
    t_cat = jnp.concatenate([t_high, t_low], axis=1)

    def rows_step(r, carry):
        parts = []
        both = [green_ref[r].astype(F32), green_ref[hk + r].astype(F32)]
        turned = [pltpu.roll(v, 64, 1) for v in both]
        for v, u in zip(both, turned):
            parts.append(jnp.where(low64, v, u))
        for v, u in zip(both, turned):
            parts.append(jnp.where(low64, u, v))
        right = jnp.concatenate(parts, axis=0).astype(BF)
        out = lax.dot_general(
            t_cat, right, (((1,), (1,)), ((), ())), preferred_element_type=F32
        )
        pages[pl.ds(r, 128, stride=PAD), :] = out
        return carry

    for r in range(hk):
        rows_step(r, 0)

    pl.semaphore_wait(plane_in, 7)

    def pack1(t):
        grp = to_group(t)
        for slot in range(8):
            q = (slot // 4) * 64 + grp * 4 + slot % 4
            start = pl.multiple_of(q * PAD, 8)
            value = pages[pl.ds(start, hk), :].astype(BF)
            packed1[grp, slot] = value.reshape(hk // 2, 2, width)

    def send(packed, landed, sent, came, t, s):
        grp, slot = to_group(t), place ^ s
        pltpu.make_async_remote_copy(
            src_ref=packed.at[grp, slot], dst_ref=landed.at[mine, place],
            send_sem=sent, recv_sem=came.at[t],
            device_id=device_of(grp, slot), device_id_type=MESH,
        ).start()

    def send1(i, carry):
        for u in range(1):
            pack1(i * 1 + u)
        for s in (6, 2, 7, 3, 4, 5, 1, 0):
            for u in range(1):
                send(packed1, landed1, ssem1, rsem1, i * 1 + u, s)
        return carry

    lax.fori_loop(0, 15, send1, 0)
    pack1(15)
    for s in (6, 2, 7, 3, 4, 5, 1):
        send(packed1, landed1, ssem1, rsem1, 15, s)
    own1 = pltpu.make_async_copy(packed1.at[mine, place], landed1.at[mine, place], rsem1.at[15])
    own1.start()

    for fetch in fetches[2:]:
        fetch.wait()
    zeros = jnp.zeros((64, 128), F32)
    basis = basis_ref[...]
    wide = jnp.concatenate(
        [jnp.concatenate([basis, zeros], axis=1), jnp.concatenate([zeros, basis], axis=1)], axis=0
    )
    high, low = split(wide)
    tb[0:128, :] = high
    tb[128:256, :] = low
    proj = proj_ref[...].T
    blank = jnp.zeros((128, 64), F32)
    left, right = jnp.concatenate([proj, blank], axis=1), jnp.concatenate([blank, proj], axis=1)
    for offset, piece in ((0, left), (128, right)):
        high, low = split(piece)
        pb[offset:offset + 128, :] = high
        pb[256 + offset:256 + offset + 128, :] = low
    pt[0:128, :] = left
    for grp in range(16):
        for h in range(2):
            pt[pl.ds(128 + grp * 8 + h * 4, 4), :] = pt[pl.ds(h * 64 + grp * 4, 4), :]
    left = pt[128:256, :]
    right = pltpu.roll(left, 64, 1)
    for offset, piece in ((0, left), (128, right)):
        high, low = split(piece)
        pq[offset:offset + 128, :] = high
        pq[256 + offset:256 + offset + 128, :] = low
    memk = memk_ref[...]
    blank = jnp.zeros((64, 64), F32)
    wide = jnp.concatenate(
        [jnp.concatenate([memk, blank], axis=1), jnp.concatenate([blank, memk], axis=1)], axis=0
    )
    high, low = split(wide)
    kb[0:128, :] = high
    kb[128:256, :] = low
    scale = 1.0 / w_raw.shape[0]

    def widen(i, carry):
        value = w_raw[pl.ds(pl.multiple_of(i * 48, 16), 48), :].astype(F32) * scale
        wre_full[pl.ds(i, 48, stride=48), :] = value[:, :128]
        wim_full[pl.ds(i, 48, stride=48), :] = value[:, 128:]
        return carry

    lax.fori_loop(0, 48, widen, 0)
    xbuf[...] = jnp.zeros_like(xbuf)

    def arrive1(t, carry):
        grp = from_group(t)

        ref = landed1.at[grp]
        pltpu.make_async_copy(ref, ref, rsem1.at[t]).wait()

        for i in range(4):
            v0 = landed1[grp, i].reshape(hk, width).astype(F32)
            v1 = landed1[grp, 4 + i].reshape(hk, width).astype(F32)
            xbuf[i * 2 * PAD:i * 2 * PAD + hk, :] = jnp.where(low32, v0, pltpu.roll(v1, 32, 1))
            xbuf[i * 2 * PAD + PAD:i * 2 * PAD + PAD + hk, :] = jnp.where(
                low32, pltpu.roll(v0, 96, 1), v1
            )
        value = xbuf[...]
        stacked = jnp.concatenate([value.astype(BF), times_i(value).astype(BF)], axis=0)
        out = dot(yf_ref[...], stacked)
        for u in range(3):
            ytab[pl.ds(grp * 3 + u, 48, stride=48), :] = out[u * 48:u * 48 + 48]
        return carry

    lax.fori_loop(0, 16, arrive1, 0)

    swap(1).start()

    together = 24

    def along_x(values, sign):
        done = []
        for u in range(0, len(values), 2 * 3):
            sides = [
                jnp.concatenate([v.astype(BF) for v in values[at:at + 3]], axis=0)
                for at in (u, u + 3)
            ]
            out = dot(xf_ref[...], jnp.concatenate(sides, axis=1))
            for v in range(2):
                for at in range(0, 96 * 3, 96):
                    even = out[at:at + 48, v * 128:v * 128 + 128]
                    odd = out[at + 48:at + 96, v * 128:v * 128 + 128]
                    done.append(even + pltpu.roll(odd, 64, 1) * (minus_low * sign))
        return done


    def distances(step, carry):
        near_in = along_x(
            [ytab[pl.ds(pl.multiple_of((step * together + u) * 48, 8), 48), :] for u in range(together)],
            1.0,
        )
        near_in = [v.astype(BF) for v in near_in]
        near_in = jnp.concatenate(near_in, axis=0)
        near = dot(jnp.concatenate([near_in, near_in], axis=1), tb[...])
        far_parts = []
        for u in range(together):
            ry = step * together + u
            w_re = wre_full[pl.ds(pl.multiple_of(ry * 48, 8), 48), :]
            w_im = wim_full[pl.ds(pl.multiple_of(ry * 48, 8), 48), :]
            n_re, n_im = near[u * 48:u * 48 + 48, :128], near[u * 48:u * 48 + 48, 128:]
            far_re = -(n_re * w_im + n_im * w_re)
            far_im = n_re * w_re - n_im * w_im
            far_parts.append(jnp.concatenate([far_re.astype(BF), far_im.astype(BF)], axis=1))
        far = jnp.concatenate(far_parts, axis=0)
        home = dot(far, pb[0:256, :]) + dot(far, pb[256:512, :])
        back = along_x([home[u * 48:u * 48 + 48, :] for u in range(together)], -1.0)
        for u in range(together):
            utab[pl.ds(pl.multiple_of((step * together + u) * 48, 8), 48), :] = back[u]
        return carry

    lax.fori_loop(0, 48 // together, distances, 0)

    def pack2(t):
        grp = to_group(t)
        value = jnp.concatenate(
            [utab[pl.ds(grp * 3 + u, 48, stride=48), :] for u in range(3)], axis=0
        )
        stacked = jnp.concatenate([value.astype(BF), times_i(value).astype(BF)], axis=0)
        out = dot(yi_ref[...], stacked)
        for i in range(4):
            v0 = out[i * 2 * PAD:i * 2 * PAD + PAD]
            v1 = out[i * 2 * PAD + PAD:i * 2 * PAD + 2 * PAD]
            first = jnp.where(low32, v0, pltpu.roll(v1, 32, 1))
            second = jnp.where(low32, pltpu.roll(v0, 96, 1), v1)
            packed2[grp, i] = first[:hk].astype(BF).reshape(hk // 2, 2, width)
            packed2[grp, 4 + i] = second[:hk].astype(BF).reshape(hk // 2, 2, width)

    def send2(i, carry):
        for u in range(1):
            pack2(i * 1 + u)
        for s in (6, 2, 7, 3, 4, 5, 1, 0):
            for u in range(1):
                send(packed2, landed2, ssem2, rsem2, i * 1 + u, s)
        return carry

    lax.fori_loop(0, 15, send2, 0)
    pack2(15)
    for s in (6, 2, 7, 3, 4, 5, 1):
        send(packed2, landed2, ssem2, rsem2, 15, s)
    own2 = pltpu.make_async_copy(packed2.at[mine, place], landed2.at[mine, place], rsem2.at[15])
    own2.start()

    swap(0).wait()
    swap(1).wait()
    mine_at = pl.multiple_of(half * rows_m, 32)
    other_at = pl.multiple_of((1 - half) * rows_m, 32)

    def build(k, carry):
        for ref, at in ((green_ref, mine_at), (partner, other_at)):
            value = ref[k]
            turned = (pltpu.roll(value.astype(F32), 64, 1) * -minus_low).astype(BF)
            gmat[k, pl.ds(at, rows_m), :] = turned
            gmat[k, pl.ds(64 + at, rows_m), :] = value
        return carry

    lax.fori_loop(0, count_k, build, 0)

    def arrive2(t, carry):
        grp = from_group(t)

        ref = landed2.at[grp]
        pltpu.make_async_copy(ref, ref, rsem2.at[t]).wait()

        for slot in range(8):
            value = landed2[grp, slot].reshape(hk, width).astype(F32)
            start = pl.multiple_of((grp * 8 + slot) * PAD, 8)
            pages[pl.ds(start, hk), :] = value
        return carry

    lax.fori_loop(0, 16, arrive2, 0)

    for r in range(hk):
        value = pages[pl.ds(r, 128, stride=PAD), :].T.astype(BF)
        for k2 in range(2):
            amat[(k2 * hk + r) * rows_m:(k2 * hk + r + 1) * rows_m, 0:128] = value[
                k2 * 32:k2 * 32 + 32
            ]
            amat[(k2 * hk + r) * rows_m:(k2 * hk + r + 1) * rows_m, 128:256] = value[
                64 + k2 * 32:64 + k2 * 32 + 32
            ]

    def coeffs(i, carry):
        at = pl.multiple_of(i * 1152, 32)
        value = amat[pl.ds(at, 1152), :]
        sigma = (dot(value, pq[0:256, :]) + dot(value, pq[256:512, :])).astype(BF)
        both_ref[:, :, 0:128] = sigma.reshape(36, rows_m, width).astype(F32)
        skm[pl.ds(at, 1152), :] = dot(jnp.concatenate([sigma, sigma], axis=1), kb[...]).astype(BF)
        for u in range(0, 36, 2):
            pair = dot(
                skm[u * 32:u * 32 + 64, :], jnp.concatenate([gmat[u], gmat[u + 1]], axis=1)
            )
            for k, memory in ((u, pair[:rows_m, :128]), (u + 1, pair[rows_m:, 128:])):
                turned = gmat[k, pl.ds(mine_at, rows_m), :].astype(F32)
                own = green_ref[k].astype(F32)
                energy = energy_ref[orbital, k]
                both_ref[k, :, 128:256] = own + STEP_SIZE * (energy * turned + memory)
        return carry

    lax.fori_loop(0, count_k // 36, coeffs, 0)

    ref = landed1.at[pl.ds(0, 15)]
    pltpu.make_async_copy(ref, ref, ssem1).wait()
    ref = landed1.at[0, pl.ds(0, 7)]
    pltpu.make_async_copy(ref, ref, ssem1).wait()
    ref = landed2.at[pl.ds(0, 15)]
    pltpu.make_async_copy(ref, ref, ssem2).wait()
    ref = landed2.at[0, pl.ds(0, 7)]
    pltpu.make_async_copy(ref, ref, ssem2).wait()


def on_device(green_coeff, screened, band_energy, time_basis, projector, memory_kernel):
    total_k = screened.shape[0]
    tables = [jnp.asarray(t, BF) for t in phase_tables(48, green_coeff.shape[0], 4)]
    vmem = pl.BlockSpec(memory_space=pltpu.VMEM)
    dma = pltpu.SemaphoreType.DMA
    message = (16, 8, 9, 2, 128)
    out = pltpu.VMEM((36, 32, 256), F32)
    both = pl.pallas_call(
        kernel,
        out_shape=out,
        in_specs=[pl.BlockSpec(memory_space=pl.ANY)] * 10,
        out_specs=vmem,
        scratch_shapes=[
            pltpu.VMEM(green_coeff.shape, BF),
            pltpu.VMEM((total_k, 256), BF),
            pltpu.SMEM((2, green_coeff.shape[0]), F32),
            pltpu.VMEM(time_basis.shape, F32),
            pltpu.VMEM(time_basis.shape, F32),
            pltpu.VMEM(memory_kernel.shape, F32),
            *[pltpu.VMEM(t.shape, BF) for t in tables],
            dma((10,)),
            pltpu.SemaphoreType.REGULAR,
            pltpu.VMEM((total_k + 48, 128), F32),
            pltpu.VMEM((total_k + 48, 128), F32),
            pltpu.VMEM((129 * PAD, 128), F32),
            pltpu.VMEM(message, BF),
            pltpu.VMEM(message, BF),
            pltpu.VMEM(message, BF),
            pltpu.VMEM(message, BF),
            pltpu.VMEM((total_k + 48, 128), F32),
            pltpu.VMEM((total_k + 48, 128), F32),
            pltpu.VMEM((8 * PAD, 128), F32),
            pltpu.VMEM((256, 256), BF),
            pltpu.VMEM((512, 128), BF),
            pltpu.VMEM((512, 128), BF),
            pltpu.VMEM((256, 128), BF),
            pltpu.VMEM((256, 128), F32),
            pltpu.VMEM(green_coeff.shape, BF),
            pltpu.VMEM((36, 128, 128), BF),
            pltpu.VMEM((1152, 256), BF),
            pltpu.VMEM((1152, 128), BF),
            dma, dma, dma((16,)), dma, dma((16,)), dma((2,)), dma((2,)),
        ],
        compiler_params=pltpu.CompilerParams(
            collective_id=0, has_side_effects=True, vmem_limit_bytes=60 * 2**20
        ),
    )(
        green_coeff,
        screened.reshape(total_k, 256),
        band_energy.T,
        time_basis,
        projector.T,
        memory_kernel,
        *tables,
    )
    return both[:, :, :128].astype(BF), both[:, :, 128:].astype(BF)


def solution(mesh):
    return jax.shard_map(
        on_device,
        mesh=mesh,
        in_specs=(P("ka", "ot", None), P(None, ("ot", "ka"), None), P("ka", None), P(), P(), P()),
        out_specs=(P("ka", "ot", None), P("ka", "ot", None)),
        check_vma=False,
    )
```
